256 devices in a mesh: blk: 64 (over y, x, z_hi), ma: 4 (over z_lo, core).
Axes of the slice: x: 4, y: 4, z: 8 (z_hi: 4, z_lo: 2; z = z_hi * 2 + z_lo), core: 2. Of those that a mesh axis runs over, the one named last changes fastest.
Arguments:
- white_noise: float32 [2560, 2, 2560], P(('ma', 'blk')), may hold values from -6 to 6
- amplitude: float32 [2560], replicated, may hold values from 0.002 to 0.015
- legendre: bfloat16 [128, 2560, 2560], P('blk', 'ma'), may hold values from -0.125 to 0.125
- order_of_slot: int32 [2560], replicated, may hold values from 0 to 2559, as said below
- counts: int32 [256, 8192], P(('blk', 'ma')), may hold values from 0 to 7
- survey_mask: int32 [256, 8192], P(('blk', 'ma')), may hold values from 0 to 1, as said below
Outputs:
- gradient: float32 [2560, 2, 2560], P(('ma', 'blk'))
The draws below stay inside these ranges and needn't reach their ends.
Inputs may be any that keep to these rules, and one draw needn't show every extreme that they name: `order_of_slot`: a permutation of 0 to 2559 in which slots 2k and 2k+1 hold the orders m and 2559-m. `survey_mask`: every cycle row has at least one pixel equal to 1.
All inputs are finite; a program needn't handle non-finite values.
Results may differ from the reference program's by a relative error of at most 0.004.
Values may be sent and summed in bfloat16 or wider, within the bound.
A program may use at most 128 MiB of HBM per device.

```python
import math
import jax
import jax.numpy as jnp
from jax import lax

L = 2560
M = 2560
NPHI = 8192
RH = 2
NHN = 128
NR = 256
N_BLK = 64


def draw_order_of_slot(key, part):
    key = jax.random.fold_in(key, 11)
    first_key, second_key = jax.random.split(key)
    half_count = M // 2
    paired = jax.random.permutation(first_key, half_count).astype(jnp.int32)
    flipped = jax.random.randint(second_key, (half_count,), 0, 2).astype(jnp.int32)
    lower = jnp.where(flipped == 1, M - 1 - paired, paired)
    upper = M - 1 - lower
    return jnp.stack([lower, upper], axis=1).reshape(M).astype(jnp.int32)


def draw_counts(key, part):
    key = jax.random.fold_in(key, 23)
    row_index = jnp.arange(NR, dtype=jnp.int32)[:, None]
    ceiling = 3 + 6 * row_index // NR
    raw_bits = jax.random.randint(key, (NR, NPHI), 0, 1 << 20)
    return (raw_bits % ceiling).astype(jnp.int32)


def draw_survey_mask(key, part):
    key = jax.random.fold_in(key, 37)
    first_key, second_key = jax.random.split(key)
    row_index = jnp.arange(NR, dtype=jnp.int32)[:, None]
    column = jnp.arange(NPHI, dtype=jnp.int32)[None, :]
    level = 300 + 650 * row_index // NR
    raw_bits = jax.random.randint(first_key, (NR, NPHI), 0, 1000)
    anchor = jax.random.randint(second_key, (NR, 1), 0, NPHI)
    return jnp.where((raw_bits < level) | (column == anchor), 1, 0).astype(jnp.int32)


def block_levels(key, shape, pieces, smallest, largest):
    factor_of = 1.0
    for dim, blocks in pieces:
        draws = jax.random.uniform(jax.random.fold_in(jax.random.fold_in(key, 6), dim), (blocks,), jnp.float32, smallest / len(pieces), largest / len(pieces))
        factor_of = factor_of * jnp.repeat(jnp.exp(draws), shape[dim] // blocks).reshape((-1,) + (1,) * (len(shape) - 1 - dim))
    return factor_of


def noise(key, shape, spread, most, cuts=(), kind=jnp.bfloat16):
    level = block_levels(key, shape, cuts, -0.22, 0.18) if cuts else 1.0
    values = jax.random.normal(key, shape, jnp.float32) * spread * level
    return jnp.minimum(jnp.maximum(values, -most), most).astype(kind)


def setup_inputs(seed: int = 0) -> dict:
    arg_keys = jax.random.split(jax.random.key(seed), 7)
    white_noise = noise(arg_keys[0], (M, 2, L), 1.0, 6.0, ((0, 256),), jnp.float32)
    amplitude = jnp.clip(jnp.exp(jax.random.uniform(arg_keys[1], (L,), jnp.float32, math.log(0.002), math.log(0.015))), 0.002, 0.015)
    legendre = noise(arg_keys[2], (NHN, M, L), L ** -0.5, 0.125, ((0, 64), (1, 4)))
    order_of_slot = draw_order_of_slot(jax.random.fold_in(arg_keys[6], 71), 0)
    counts = draw_counts(jax.random.fold_in(arg_keys[6], 71), 0)
    survey_mask = draw_survey_mask(jax.random.fold_in(arg_keys[6], 71), 0)
    return dict(white_noise=white_noise, amplitude=amplitude, legendre=legendre, order_of_slot=order_of_slot, counts=counts, survey_mask=survey_mask)


def parity_signs(orders, degrees):
    degree = jnp.arange(degrees, dtype=jnp.int32)
    return jnp.where((degree[None, :] + orders[:, None]) % 2 == 0, 1.0, -1.0).astype(jnp.float32)


def reference(white_noise, amplitude, legendre, order_of_slot, counts, survey_mask):
    orders = order_of_slot.astype(jnp.int32)
    degree = jnp.arange(L, dtype=jnp.int32)
    own_keep = degree[None, :] >= orders[:, None]
    parity_sign = parity_signs(orders, L)
    harmonics = jnp.where(own_keep[:, None, :], amplitude[None, None, :] * white_noise, 0.0).astype(jnp.bfloat16)
    harmonics = lax.optimization_barrier(harmonics)
    base = harmonics.astype(jnp.float32)
    stacked = jnp.concatenate([base, base * parity_sign[:, None, :]], axis=1)
    band_tables = legendre.reshape(N_BLK, RH, M, L)

    def synthesize(table_band):
        return jnp.einsum('nsl,skl->kns', table_band.astype(jnp.float32), stacked)

    fourier = lax.map(synthesize, band_tables)
    fourier = fourier.reshape(N_BLK, 2, 2, RH, M).transpose(2, 0, 1, 3, 4).reshape(2, NR, M)

    row_index = jnp.arange(NR, dtype=jnp.int32)
    north_index = (row_index // (2 * RH)) * RH + row_index % RH
    parity = north_index % 2
    weight_m = jnp.where(orders == 0, 1.0, 2.0).astype(jnp.float32)
    phase_turn = (orders[None, :] * parity[:, None]) % (2 * NPHI)
    phase_angle = jnp.pi * phase_turn.astype(jnp.float32) / NPHI
    cos_phase = jnp.cos(phase_angle)
    sin_phase = jnp.sin(phase_angle)
    spec_re = weight_m * (fourier[0] * cos_phase - fourier[1] * sin_phase)
    spec_im = weight_m * (fourier[0] * sin_phase + fourier[1] * cos_phase)
    full_re = jnp.zeros((NR, NPHI), jnp.float32).at[:, orders].set(spec_re)
    full_im = jnp.zeros((NR, NPHI), jnp.float32).at[:, orders].set(spec_im)
    log_density = jnp.real(jnp.fft.ifft(lax.complex(full_re, full_im), axis=1)) * NPHI

    inside = survey_mask.astype(jnp.float32)
    number = counts.astype(jnp.float32)
    weight = inside * jnp.exp(log_density)
    weight_total = jnp.sum(weight)
    count_total = jnp.sum(inside * number)
    residual = inside * (number - count_total * weight / weight_total)

    spectrum = jnp.fft.fft(lax.complex(residual, jnp.zeros_like(residual)), axis=1)
    picked = spectrum[:, orders]
    modes_re = jnp.real(picked)
    modes_im = jnp.imag(picked)
    back_re = weight_m * (modes_re * cos_phase + modes_im * sin_phase)
    back_im = weight_m * (modes_im * cos_phase - modes_re * sin_phase)
    backward = jnp.stack([back_re, back_im]).astype(jnp.bfloat16)
    backward = lax.optimization_barrier(backward).astype(jnp.float32)
    backward = backward.reshape(2, N_BLK, 2, RH, M).transpose(1, 0, 2, 3, 4).reshape(N_BLK, 4, RH, M)

    def analyse(total_sum, scan_item):
        table_band, back_part = scan_item
        return total_sum + jnp.einsum('nsl,kns->skl', table_band.astype(jnp.float32), back_part), None

    summed, _ = lax.scan(analyse, jnp.zeros((M, 4, L), jnp.float32), (band_tables, backward))
    summed = summed.reshape(M, 2, 2, L)
    combined = summed[:, :, 0] + parity_sign[:, None, :] * summed[:, :, 1]
    return jnp.where(own_keep[:, None, :], amplitude[None, None, :] * combined, 0.0)
```

```python
import functools

import jax
import jax.numpy as jnp
import numpy as np
from jax import lax
from jax.experimental import pallas as pl
from jax.experimental.pallas import tpu as pltpu
from jax.sharding import PartitionSpec as P

MESH = pl.DeviceIdType.MESH
F32 = jnp.float32
BF16 = jnp.bfloat16
EXACT = lax.Precision.HIGHEST

SIDE = 4
OWN = 5
PAIRS = 80
XT, YT = 11, 10
LANES = (XT * 128, YT * 128)


def nt(a, b, precision=None):
    return lax.dot_general(
        a, b, (((1,), (1,)), ((), ())), preferred_element_type=F32, precision=precision
    )


def nn(a, b, precision=None):
    return lax.dot_general(
        a, b, (((1,), (0,)), ((), ())), preferred_element_type=F32, precision=precision
    )


def selection_tables():
    pick_x = np.zeros((2, 160, 192), np.float32)
    for odd in range(2):
        for y in range(SIDE):
            for i in range(20):
                for ab in range(2):
                    pick_x[odd, ab * 80 + y * 20 + i, y * 48 + odd * 8 + 2 * i + ab] = 1
    pick_y = np.zeros((160, 160), np.float32)
    for i in range(80):
        for ab in range(2):
            pick_y[ab * 80 + i, 2 * i + ab] = 1
    flip = np.fliplr(np.eye(256, dtype=np.float32))
    spread = np.zeros((512, 480), np.float32)
    for dev in range(16):
        for j in range(3):
            for c in range(2):
                for k in range(OWN):
                    spread[dev * 32 + (j * 2 + c) * OWN + k, (j * 2 + c) * 80 + dev * OWN + k] = 1
    alt = np.where(np.arange(128) % 2 == 0, 1.0, -1.0)
    expand = np.zeros((32, 1024), np.float32)
    for r in range(4):
        for e in range(4):
            col = ((r % 2) * 4 + e) * 128
            expand[r * 8 + e, col : col + 128] = 1.0 if r < 2 else alt
    lane_sum = np.zeros((8, 128), np.float32)
    lane_sum[0] = 1
    lane_sum[1] = alt
    eye = np.eye(128, dtype=np.float32)
    return [
        np.asarray(t, jnp.bfloat16)
        for t in (pick_x, pick_y, flip, spread, spread.T.copy(), expand, lane_sum, eye)
    ]


def dft_tables():
    p = np.arange(40)
    q = np.arange(64)
    u = np.arange(64)
    v = np.arange(128)
    synth, turn_a, turn_b, back_re, back_im, gather = [], [], [], [], [], []
    for h in range(2):
        coarse = 2 * np.pi * ((p[:, None] * (2 * v[None, :] + h)) % 256) / 256
        c, s = np.cos(coarse), np.sin(coarse)
        top = np.concatenate([c.T, -s.T], 1)
        low = np.concatenate([s.T, c.T], 1)
        synth.append(np.concatenate([top, low], 0))
        turn = 2 * np.pi * ((q[None, :] * (2 * v[:, None] + h)) % 16384) / 16384
        tc, ts = np.cos(turn), np.sin(turn)
        turn_a.append(np.concatenate([tc, ts], 1))
        turn_b.append(np.concatenate([-ts, tc], 1))
        back_re.append(tc.T.copy())
        back_im.append(ts.T.copy())
        gather.append(
            np.concatenate([np.concatenate([c, s], 1), np.concatenate([-s, c], 1)], 0)
        )
    fine = 2 * np.pi * ((q[None, :] * u[:, None]) % 64) / 64
    fc, fs = np.cos(fine), np.sin(fine)
    fine_out = np.concatenate([fc, -fs], 1)
    fine_in = np.concatenate([fc.T, -fs.T], 0)
    weight = np.full((80, 128), 2.0)
    weight[0, 0] = weight[40, 0] = weight[0, 64] = weight[40, 64] = 1.0
    return [
        np.asarray(t, np.float32)
        for t in (
            np.stack(synth),
            np.stack(turn_a),
            np.stack(turn_b),
            np.stack(back_re),
            np.stack(back_im),
            np.stack(gather),
            fine_out,
            fine_in,
            weight,
        )
    ]


def kernel(
    leg, harm, thr, ordv, cnt, msk,
    pick_x, pick_y, flip, spread, spread_t, expand, lane_sum, eye,
    synth, turn_a, turn_b, back_re, back_im, gather, fine_out, fine_in, weight,
    out,
    lg, ls_x, ls_y, lr_x, lr_y, hg1, hg, hst, accs, fsend, frecv, pt, qt,
    bsend, brecv, psend, precv, coef, gst, gs1, gr1, gs2, gr2,
    lg_sem, ls_sem, lrecv_sem, h1s, h1r, h2s, h2r, fs_sem, fr_sem, bs_sem, br_sem,
    ps_sem, pr_sem, g1s, g1r, g2s, g2r,
):
    b = lax.axis_index("blk")
    g = lax.axis_index("ma")
    y, x, z = b // 16, (b // 4) % 4, b % 4
    pending = []

    def at(yy, xx, zz, gg):
        return (yy * 16 + xx * 4 + zz, gg)

    def shift(v, d):
        return lax.rem(v + d, 4) if d else v

    def remote(src, dst, ssem, rsem, dev):
        return pltpu.make_async_remote_copy(
            src_ref=src, dst_ref=dst, send_sem=ssem, recv_sem=rsem, device_id=dev, device_id_type=MESH
        )

    def send(src, dst, ssem, rsem, dev):
        c = remote(src, dst, ssem, rsem, dev)
        c.start()
        pending.append(c)

    peers = []
    for dx in range(4):
        for dg in range(4):
            if dx or dg:
                peers.append((0, dx, 0, dg))
    for dy in range(1, 4):
        for dg in range(4):
            peers.append((dy, 0, 0, dg))
    for dy in range(4):
        for dz in range(1, 4):
            peers.append((dy, 0, dz, 0))
    barrier = pltpu.get_barrier_semaphore()
    for dy, dx, dz, dg in peers:
        pl.semaphore_signal(
            barrier, inc=1, device_id=at(shift(y, dy), shift(x, dx), shift(z, dz), shift(g, dg)),
            device_id_type=MESH,
        )

    order = (1, 3, 2, 0)
    loads = {}
    for d in order:
        yy = shift(y, d)
        rows = pl.ds(pl.multiple_of(yy * 160, 32), 160)
        for n in range(2):
            c = pltpu.make_async_copy(leg.at[n, rows], lg.at[n, rows], lg_sem.at[n, d])
            c.start()
            loads[d, n] = c

    accs[...] = jnp.zeros_like(accs)
    gst[...] = jnp.zeros_like(gst)

    pl.semaphore_wait(barrier, len(peers))

    for m in range(2):
        hg1[m, z] = harm[m]
    for d in (1, 3, 2):
        send(harm, hg1.at[:, z], h1s.at[d], h1r.at[z], at(y, x, shift(z, d), g))

    def pack(mode, dest, n):
        t_all = thr[mode, dest]
        wide = jnp.concatenate([t_all, t_all - 128], axis=1)
        if mode == 0:
            start = (dest // 2) * 80 + (dest % 2) * 32
            sel = pick_x[dest % 2]
            buf = ls_x.at[dest, n]

            def columns(c0, width):
                return jnp.concatenate(
                    [
                        lg[n, pl.ds(pl.multiple_of(k * 160 + start, 16), 48), c0 : c0 + width]
                        for k in range(4)
                    ],
                    axis=0,
                )
        else:
            sel = pick_y[...]
            buf = ls_y.at[dest, n]

            def columns(c0, width):
                return lg[n, pl.ds(pl.multiple_of(dest * 160, 32), 160), c0 : c0 + width]

        even, odd = sel[0:80], sel[80:160]

        def a_part(tile, tiles):
            return nn(even, columns(tile * 128, tiles * 128))

        def b_part(tile, tiles):
            part = nn(odd, columns(tile * 128, tiles * 128)).astype(BF16)
            f = flip[...] if tiles == 2 else flip[128:256, 0:128]
            return nn(part, f)

        first, last = (0, XT) if mode == 0 else (XT, XT + YT)
        t = first
        while t < last:
            o = (t - first) * 128
            if t == 0:
                buf[:, o : o + 128] = b_part(19, 1).astype(BF16)
                t += 1
            elif t == 19:
                mix = jnp.where(t_all <= 128 * t, a_part(t - 1, 1), b_part(0, 1))
                buf[:, o : o + 128] = mix.astype(BF16)
                buf[:, o + 128 : o + 256] = a_part(t, 1).astype(BF16)
                t += 2
            else:
                mix = jnp.where(wide <= 128 * t, a_part(t - 1, 2), b_part(18 - t, 2))
                buf[:, o : o + 256] = mix.astype(BF16)
                t += 2

    send_bufs, recv_bufs = (ls_x, ls_y), (lr_x, lr_y)

    def place(mode, other, r):
        return at(y, other, z, r) if mode == 0 else at(other, x, z, r)

    def mine(mode):
        return x if mode == 0 else y

    def exchange(mode, d):
        dest = shift(mine(mode), d)
        for n in range(2):
            pack(mode, dest, n)
            src, dst = send_bufs[mode].at[dest, n], recv_bufs[mode].at[mine(mode), n]
            if d:
                send(src, dst, ls_sem.at[mode, d, n], lrecv_sem.at[mode, mine(mode), n], place(mode, dest, g))
            else:
                recv_bufs[mode][mine(mode), n] = send_bufs[mode][dest, n]

    for step, d in enumerate(order):
        if step == 0:
            for n in range(2):
                loads[d, n].wait()
        exchange(1, d)
        if step == 0:
            for dd in order[1:]:
                for n in range(2):
                    loads[dd, n].wait()
        exchange(0, d)
        if step == 0:
            for dd in (1, 3, 2):
                zz = shift(z, dd)
                remote(harm, hg1.at[:, zz], h1s.at[dd], h1r.at[zz], at(y, x, zz, g)).wait_recv()
            for m in range(2):
                hg[m, y if m == 0 else x] = hg1[m]
                for dd in (1, 3, 2):
                    who = at(shift(y, dd), x, z, g) if m == 0 else at(y, shift(x, dd), z, g)
                    me = y if m == 0 else x
                    send(hg1.at[m], hg.at[m, me], h2s.at[m, dd], h2r.at[m, me], who)

    def digits(i, carry):
        o = ordv[i]
        row = jnp.concatenate([o[0:1], o[1:2]], axis=1)
        hi = row >> 6
        lo = row & 63
        pt[i] = jnp.where(
            lax.broadcasted_iota(jnp.int32, (40, 256), 0) == hi, 1.0, 0.0
        ).astype(F32)
        qt[i] = jnp.where(
            (lax.broadcasted_iota(jnp.int32, (128, 256), 0) & 63) == lo, 1.0, 0.0
        ).astype(BF16)
        return carry

    lax.fori_loop(0, 32, digits, 0)

    for m in range(2):
        for dd in (1, 3, 2):
            me = shift(y if m == 0 else x, dd)
            remote(hg1.at[m], hg.at[m, me], h2s.at[m, dd], h2r.at[m, me], at(y, x, z, g)).wait_recv()
        blocks = hg[m].reshape(512, 512)

        def unstack(i, carry):
            rows = pl.ds(pl.multiple_of(i * 80, 16), 80)
            hst[m, rows, :] = nn(spread_t[rows, :], blocks)
            return carry

        lax.fori_loop(0, 6, unstack, 0)

    def synthesize(mode, src):
        tiles = (XT, YT)[mode]
        table = recv_bufs[mode]
        own = mine(mode)

        def group(i, carry):
            r0 = pl.multiple_of(i * 16, 16)
            rows = pl.ds(r0, 16)
            limit = thr[mode, own, rows, :]
            total = [[None, None], [None, None]]
            upper = [[None, None], [None, None]]
            for t in range(tiles):
                tile = t + (0 if mode == 0 else XT)
                is_a = limit <= 128 * tile
                for c in range(2):
                    row = pl.ds(pl.multiple_of(((t // 4) * 2 + c) * 80 + r0, 16), 16)
                    h = hst[mode, row, (t % 4) * 128 : (t % 4) * 128 + 128]
                    for n in range(2):
                        v = table[src, n, rows, t * 128 : t * 128 + 128].astype(F32) * h
                        w = jnp.where(is_a, v, 0.0)
                        total[n][c] = v if t == 0 else total[n][c] + v
                        upper[n][c] = w if t == 0 else upper[n][c] + w
            for n in range(2):
                for c in range(2):
                    accs[n, 2 * c, rows, :] = upper[n][c]
                    accs[n, 2 * c + 1, rows, :] = total[n][c] - upper[n][c]
            return carry

        lax.fori_loop(0, 5, group, 0)
        sign = jnp.where((ordv[mode * 16 + own * 4 + g, 0:1, :] & 1) == 1, -1.0, 1.0)
        signs = jnp.concatenate([sign] * 4, axis=1)
        for n in range(2):
            rows = accs[n].reshape(512, 128)
            hi = rows.astype(BF16)
            lo = (rows - hi.astype(F32)).astype(BF16)
            both = nt(lane_sum[...], hi) + nt(lane_sum[...], lo)
            fsend[mode, src, n] = both[0:1]
            fsend[mode, src, n + 2] = both[1:2] * signs

    for step, d in enumerate((0, 3, 1, 2)):
        for mode in (1, 0):
            own = mine(mode)
            src = shift(own, d)
            if d:
                for n in range(2):
                    remote(
                        send_bufs[mode].at[src, n], recv_bufs[mode].at[src, n],
                        ls_sem.at[mode, d, n], lrecv_sem.at[mode, src, n], at(y, x, z, g),
                    ).wait_recv()
            synthesize(mode, src)
            for e in range(4):
                r = shift(g, e)
                if d or e:
                    send(
                        fsend.at[mode, src, r], frecv.at[mode, own, g],
                        fs_sem.at[mode, d, e], fr_sem.at[mode, own, g], place(mode, src, r),
                    )
                else:
                    frecv[mode, own, g] = fsend[mode, src, r]

    for mode in (1, 0):
        for d in range(4):
            for e in range(4):
                if d or e:
                    p, r = shift(mine(mode), d), shift(g, e)
                    remote(
                        fsend.at[mode, p, r], frecv.at[mode, p, r],
                        fs_sem.at[mode, d, e], fr_sem.at[mode, p, r], at(y, x, z, g),
                    ).wait_recv()

    h = g % 2

    def scatter(i, total):
        row = frecv[i // 16, (i // 4) % 4, i % 4]
        digit = pt[i]
        both = jnp.concatenate([digit * row[:, 0:256], digit * row[:, 256:512]], axis=0)
        hi = both.astype(BF16)
        lo = (both - hi.astype(F32)).astype(BF16)
        return total + nt(jnp.concatenate([hi, lo], axis=0), qt[i])

    full = lax.fori_loop(0, 32, scatter, jnp.zeros((160, 128), F32))
    full = (full[0:80] + full[80:160]) * weight[...]
    section = nn(synth[h], full, EXACT)
    turned = section[0:128] * turn_a[h] + section[128:256] * turn_b[h]
    log_density = nt(fine_out[...], turned, EXACT)
    inside = msk[...].astype(F32)
    number = inside * cnt[...].astype(F32)
    dens = inside * jnp.exp(log_density)
    psend[0, 0] = jnp.concatenate(
        [jnp.sum(dens, axis=0, keepdims=True), jnp.sum(number, axis=0, keepdims=True)], axis=1
    )
    precv[0, x, g] = psend[0, 0]
    for d in range(4):
        for e in range(4):
            if d or e:
                send(
                    psend.at[0, 0], precv.at[0, x, g], ps_sem.at[0, d, e], pr_sem.at[0, x, g],
                    at(y, shift(x, d), z, shift(g, e)),
                )

    first = nn(fine_in[...], jnp.concatenate([number, dens], axis=1), EXACT)
    modes = []
    for f in range(2):
        re, im = first[0:64, f * 128 : f * 128 + 128], first[64:128, f * 128 : f * 128 + 128]
        tre = re * back_re[h] + im * back_im[h]
        tim = im * back_re[h] - re * back_im[h]
        both = jnp.concatenate([tre, tim], axis=1)
        modes.append(nt(gather[h], jnp.concatenate([both, both], axis=0), EXACT) * weight[...])
    modes = jnp.concatenate(modes, axis=0)
    modes_hi = modes.astype(BF16).astype(F32)
    lane = lax.broadcasted_iota(jnp.int32, (160, 128), 1)
    modes = jnp.where(lane < 64, modes_hi, modes - modes_hi).astype(BF16)

    for d in range(4):
        for e in range(4):
            if d or e:
                xx, gg = shift(x, d), shift(g, e)
                remote(
                    psend.at[0, 0], precv.at[0, xx, gg], ps_sem.at[0, d, e], pr_sem.at[0, xx, gg],
                    at(y, x, z, g),
                ).wait_recv()
    psend[1, 0] = jnp.sum(precv[0].reshape(16, 1, 256), axis=0)
    precv[1, y, z] = psend[1, 0]
    for d in range(4):
        for e in range(4):
            if d or e:
                send(
                    psend.at[1, 0], precv.at[1, y, z], ps_sem.at[1, d, e], pr_sem.at[1, y, z],
                    at(shift(y, d), x, shift(z, e), g),
                )

    def picks(i, carry):
        rows = nn(modes, qt[i])
        digit = pt[i]
        for k in range(4):
            line = jnp.sum(rows[k * 40 : k * 40 + 40] * digit, axis=0, keepdims=True)
            for ab in range(2):
                bsend[i // 16, (i // 4) % 4, i % 4, 2 * k + ab : 2 * k + ab + 1, :] = line[
                    :, ab * 128 : ab * 128 + 128
                ]
        return carry

    lax.fori_loop(0, 32, picks, 0)

    for mode in (1, 0):
        own = mine(mode)
        for d in range(4):
            for e in range(4):
                p, gg = shift(own, d), shift(g, e)
                if d or e:
                    send(
                        bsend.at[mode, p, gg], brecv.at[mode, own, g],
                        bs_sem.at[mode, d, e], br_sem.at[mode, own, g], place(mode, p, gg),
                    )
                else:
                    brecv[mode, own, g] = bsend[mode, p, gg]

    for d in range(4):
        for e in range(4):
            if d or e:
                yy, zz = shift(y, d), shift(z, e)
                remote(
                    psend.at[1, 0], precv.at[1, yy, zz], ps_sem.at[1, d, e], pr_sem.at[1, yy, zz],
                    at(y, x, z, g),
                ).wait_recv()
    sums = jnp.sum(precv[1].reshape(16, 1, 256), axis=0)
    ratio = jnp.sum(sums[:, 128:256], axis=1, keepdims=True) / jnp.sum(
        sums[:, 0:128], axis=1, keepdims=True
    )

    def analyse(mode):
        tiles = (XT, YT)[mode]
        own = mine(mode)
        for d in range(4):
            for e in range(4):
                if d or e:
                    p, r = shift(own, d), shift(g, e)
                    remote(
                        bsend.at[mode, p, r], brecv.at[mode, p, r],
                        bs_sem.at[mode, d, e], br_sem.at[mode, p, r], at(y, x, z, g),
                    ).wait_recv()
        sign = jnp.where((ordv[mode * 16 + own * 4 + g, 0:1, :] & 1) == 1, -1.0, 1.0)
        for p in range(4):
            lines = []
            for r in range(4):
                tile = brecv[mode, p, r]
                line = tile - ratio * pltpu.roll(tile, 4, 0)
                line = jnp.where(lax.broadcasted_iota(jnp.int32, (8, 128), 0) < 4, line, 0.0)
                lines.append(line if r < 2 else line * sign)
            across = nt(eye[...], jnp.concatenate(lines, axis=0).astype(BF16))
            coef[p] = nn(across[0:80].astype(BF16), expand[...])
        table = recv_bufs[mode]

        def group(i, carry):
            r0 = pl.multiple_of(i * 16, 16)
            rows = pl.ds(r0, 16)
            limit = thr[mode, own, rows, :]
            for c in range(2):
                co = [
                    [
                        [coef[p, rows, ((n * 2 + c) * 2 + ab) * 128 : ((n * 2 + c) * 2 + ab) * 128 + 128] for ab in range(2)]
                        for n in range(2)
                    ]
                    for p in range(4)
                ]
                for t in range(tiles):
                    is_a = limit <= 128 * (t + (0 if mode == 0 else XT))
                    total = None
                    for p in range(4):
                        for n in range(2):
                            v = table[p, n, rows, t * 128 : t * 128 + 128].astype(F32) * jnp.where(
                                is_a, co[p][n][0], co[p][n][1]
                            )
                            total = v if total is None else total + v
                    row = pl.ds(pl.multiple_of(((t // 4) * 2 + c) * 80 + r0, 16), 16)
                    gst[mode, row, (t % 4) * 128 : (t % 4) * 128 + 128] = total.astype(BF16)
            return carry

        lax.fori_loop(0, 5, group, 0)
        across = y if mode == 0 else x
        for d in (1, 3, 2, 0):
            dest = shift(across, d)
            rows = pl.ds(pl.multiple_of(dest * 128, 128), 128)
            part = nn(spread[rows, :], gst[mode]).astype(BF16)
            if d:
                gs1[mode, dest] = part
                who = at(dest, x, z, g) if mode == 0 else at(y, dest, z, g)
                send(gs1.at[mode, dest], gr1.at[mode, across], g1s.at[mode, d], g1r.at[mode, across], who)
            else:
                gr1[mode, across] = part

    for mode in (1, 0):
        analyse(mode)

    for mode in (1, 0):
        across = y if mode == 0 else x
        for d in (1, 3, 2):
            src = shift(across, d)
            remote(gs1.at[mode, src], gr1.at[mode, src], g1s.at[mode, d], g1r.at[mode, src], at(y, x, z, g)).wait_recv()
        total = gr1[mode, 0].astype(F32)
        for k in range(1, 4):
            total = total + gr1[mode, k].astype(F32)
        gs2[mode] = total.astype(BF16).reshape(4, 32, 512)
        gr2[mode, z] = gs2[mode, z]
        for d in (1, 3, 2):
            dest = shift(z, d)
            send(gs2.at[mode, dest], gr2.at[mode, z], g2s.at[mode, d], g2r.at[mode, z], at(y, x, dest, g))
    for mode in (1, 0):
        for d in (1, 3, 2):
            src = shift(z, d)
            remote(gs2.at[mode, src], gr2.at[mode, src], g2s.at[mode, d], g2r.at[mode, src], at(y, x, z, g)).wait_recv()
        total = gr2[mode, 0].astype(F32)
        for k in range(1, 4):
            total = total + gr2[mode, k].astype(F32)
        out[mode] = total

    for c in pending:
        c.wait_send()


def per_device(white_noise, amplitude, legendre, order_of_slot, counts, survey_mask):
    blk = lax.axis_index("blk")
    ma = lax.axis_index("ma")
    degrees = legendre.shape[2]
    own_slots = white_noise.shape[0]
    bands = lax.axis_size("blk")
    own_orders = lax.dynamic_slice_in_dim(order_of_slot, (ma * bands + blk) * own_slots, own_slots)
    degree = jnp.arange(degrees, dtype=jnp.int32)
    own_keep = degree[None, :] >= own_orders[:, None]
    harmonics = jnp.where(own_keep[:, None, :], amplitude[None, None, :] * white_noise, 0.0).astype(BF16)
    pairs = harmonics.reshape(OWN, 2, 2, degrees)
    line = jnp.pad(pairs[:, 0], ((0, 0), (0, 0), (128, 0))) + jnp.pad(
        pairs[:, 1, :, ::-1], ((0, 0), (0, 0), (0, 128))
    )
    halves = []
    for lo, hi in ((0, LANES[0]), (LANES[0], LANES[0] + LANES[1])):
        part = jnp.pad(line[:, :, lo:hi], ((0, 0), (0, 0), (0, 1536 - (hi - lo))))
        part = part.reshape(OWN, 2, 3, 512).transpose(2, 1, 0, 3).reshape(30, 512)
        halves.append(jnp.pad(part, ((0, 2), (0, 0))))
    harm = jnp.stack(halves)

    grid = order_of_slot.reshape(4, 4, 4, 20, 2)
    by_x = grid.transpose(2, 0, 4, 1, 3).reshape(4, 4, 2, 80)
    by_y = grid.transpose(1, 0, 4, 2, 3).reshape(4, 4, 2, 80)
    ordv = jnp.stack([by_x, by_y])
    own_even = lax.dynamic_index_in_dim(ordv[:, :, :, 0], ma, axis=2, keepdims=False)
    thr = own_even[..., None] + 128 - jnp.arange(128, dtype=jnp.int32)
    ordv = jnp.pad(ordv, ((0, 0),) * 4 + ((0, 48),), constant_values=-1).reshape(32, 2, 128)

    tables = [jnp.asarray(t) for t in selection_tables() + dft_tables()]
    vmem = pl.BlockSpec(memory_space=pltpu.VMEM)
    dma = pltpu.SemaphoreType.DMA
    got = pl.pallas_call(
        kernel,
        out_shape=jax.ShapeDtypeStruct((2, 32, 512), F32),
        in_specs=[pl.BlockSpec(memory_space=pl.ANY)] + [vmem] * (5 + len(tables)),
        out_specs=vmem,
        scratch_shapes=[
            pltpu.VMEM((2, 640, 2560), BF16),
            pltpu.VMEM((4, 2, 80, LANES[0]), BF16),
            pltpu.VMEM((4, 2, 80, LANES[1]), BF16),
            pltpu.VMEM((4, 2, 80, LANES[0]), BF16),
            pltpu.VMEM((4, 2, 80, LANES[1]), BF16),
            pltpu.VMEM((2, 4, 32, 512), BF16),
            pltpu.VMEM((2, 4, 4, 32, 512), BF16),
            pltpu.VMEM((2, 480, 512), F32),
            pltpu.VMEM((2, 4, 128, 128), F32),
            pltpu.VMEM((2, 4, 4, 1, 512), F32),
            pltpu.VMEM((2, 4, 4, 1, 512), F32),
            pltpu.VMEM((32, 40, 256), F32),
            pltpu.VMEM((32, 128, 256), BF16),
            pltpu.VMEM((2, 4, 4, 8, 128), F32),
            pltpu.VMEM((2, 4, 4, 8, 128), F32),
            pltpu.VMEM((2, 1, 1, 256), F32),
            pltpu.VMEM((2, 4, 4, 1, 256), F32),
            pltpu.VMEM((4, 80, 1024), F32),
            pltpu.VMEM((2, 480, 512), BF16),
            pltpu.VMEM((2, 4, 128, 512), BF16),
            pltpu.VMEM((2, 4, 128, 512), BF16),
            pltpu.VMEM((2, 4, 32, 512), BF16),
            pltpu.VMEM((2, 4, 32, 512), BF16),
            dma((2, 4)),
            dma((2, 4, 2)),
            dma((2, 4, 2)),
            dma((4,)),
            dma((4,)),
            dma((2, 4)),
            dma((2, 4)),
            dma((2, 4, 4)),
            dma((2, 4, 4)),
            dma((2, 4, 4)),
            dma((2, 4, 4)),
            dma((2, 4, 4)),
            dma((2, 4, 4)),
            dma((2, 4)),
            dma((2, 4)),
            dma((2, 4)),
            dma((2, 4)),
        ],
        compiler_params=pltpu.CompilerParams(
            collective_id=0, has_side_effects=True, vmem_limit_bytes=50 * 1024 * 1024
        ),
        name="survey",
    )(
        legendre, harm, thr, ordv, counts.reshape(64, 128), survey_mask.reshape(64, 128), *tables
    )
    lines = got[:, :30].reshape(2, 3, 2, OWN, 512).transpose(0, 3, 2, 1, 4).reshape(2, OWN, 2, 1536)
    line = jnp.concatenate([lines[0, :, :, : LANES[0]], lines[1, :, :, : LANES[1]]], axis=2)
    summed = jnp.stack([line[:, :, 128:], line[:, :, degrees - 1 :: -1]], axis=1)
    summed = summed.reshape(own_slots, 2, degrees)
    return jnp.where(own_keep[:, None, :], amplitude[None, None, :] * summed, 0.0)


def solution(mesh):
    placed = (
        P(("ma", "blk"), None, None),
        P(),
        P("blk", "ma", None),
        P(),
        P(("blk", "ma"), None),
        P(("blk", "ma"), None),
    )
    return jax.shard_map(
        per_device,
        mesh=mesh,
        in_specs=placed,
        out_specs=P(("ma", "blk"), None, None),
        check_vma=False,
    )
```

```python
import functools

import jax
import jax.numpy as jnp
import numpy as np
from jax import lax
from jax.experimental import pallas as pl
from jax.experimental.pallas import tpu as pltpu
from jax.sharding import PartitionSpec as P

MESH = pl.DeviceIdType.MESH
F32 = jnp.float32
BF16 = jnp.bfloat16

SIDE = 4
OWN = 5
PAIRS = 80
XT, YT = 12, 9
PIECE = (XT // 3, YT // 3)
LANES = (XT * 128, YT * 128)


def nt(a, b):
    return lax.dot_general(
        a, b, (((1,), (1,)), ((), ())), preferred_element_type=F32
    )


def nn(a, b):
    return lax.dot_general(
        a, b, (((1,), (0,)), ((), ())), preferred_element_type=F32
    )


def selection_tables():
    flip = np.fliplr(np.eye(256, dtype=np.float32))
    spread = np.zeros((512, 480), np.float32)
    for dev in range(16):
        for j in range(3):
            for c in range(2):
                for k in range(OWN):
                    spread[dev * 32 + j * 10 + 2 * k + c, (j * 2 + c) * 80 + dev * OWN + k] = 1
    alt = np.where(np.arange(128) % 2 == 0, 1.0, -1.0)
    expand = np.zeros((32, 1024), np.float32)
    for r in range(4):
        for e in range(4):
            col = ((r % 2) * 4 + e) * 128
            expand[r * 8 + e, col : col + 128] = 1.0 if r < 2 else alt
    lane_sum = np.zeros((8, 256), np.float32)
    lane_sum[0] = 1
    lane_sum[1] = np.concatenate([alt, alt])
    eye = np.eye(128, dtype=np.float32)
    place = np.zeros((640, 2, 4, 2, 128), np.float32)
    for yy in range(SIDE):
        for xx in range(SIDE):
            for i in range(20):
                for ab in range(2):
                    slot = 2 * (yy * 80 + xx * 20 + i) + ab
                    place[slot, 0, xx, ab, yy * 20 + i] = 1
                    place[slot, 1, yy, ab, xx * 20 + i] = 1
    place = place.reshape(640, 2048)
    column = np.zeros((16, 1024), np.float32)
    for i in range(8):
        column[i, i * 128 : i * 128 + 128] = 64
        column[8 + i, i * 128 : i * 128 + 128] = 1
    return [
        np.asarray(t, jnp.bfloat16)
        for t in (place, eye, column, flip, spread, spread.T.copy(), expand, lane_sum)
    ]


def dft_tables():
    p = np.arange(40)
    q = np.arange(64)
    u = np.arange(64)
    v = np.arange(128)
    synth, turn_a, turn_b, back_re, back_im, gather = [], [], [], [], [], []
    for h in range(2):
        coarse = 2 * np.pi * ((p[:, None] * (2 * v[None, :] + h)) % 256) / 256
        c, s = np.cos(coarse), np.sin(coarse)
        top = np.concatenate([c.T, -s.T], 1)
        low = np.concatenate([s.T, c.T], 1)
        synth.append(np.concatenate([top, low], 0))
        turn = 2 * np.pi * ((q[None, :] * (2 * v[:, None] + h)) % 16384) / 16384
        tc, ts = np.cos(turn), np.sin(turn)
        turn_a.append(np.concatenate([tc, ts], 1))
        turn_b.append(np.concatenate([-ts, tc], 1))
        back_re.append(tc.T.copy())
        back_im.append(ts.T.copy())
        gather.append(
            np.concatenate([np.concatenate([c, s], 1), np.concatenate([-s, c], 1)], 0)
        )
    fine = 2 * np.pi * ((q[None, :] * u[:, None]) % 64) / 64
    fc, fs = np.cos(fine), np.sin(fine)
    fine_out = np.concatenate([fc, -fs], 1)
    fine_in = np.concatenate([fc.T, -fs.T], 0)
    weight = np.full((80, 128), 2.0)
    weight[0, 0] = weight[40, 0] = weight[0, 64] = weight[40, 64] = 1.0

    def split(t):
        t = np.asarray(t, np.float32)
        hi = t.astype(jnp.bfloat16)
        lo = (t - hi.astype(np.float32)).astype(jnp.bfloat16)
        return np.concatenate([hi, lo, hi], axis=-1)

    return [
        split(np.stack(synth)),
        np.stack(turn_a).astype(np.float32),
        np.stack(turn_b).astype(np.float32),
        np.stack(back_re).astype(np.float32),
        np.stack(back_im).astype(np.float32),
        split(np.stack(gather)),
        split(fine_out),
        split(fine_in),
        weight.astype(np.float32),
    ]


OPERANDS = (
    "order", "place", "eye", "column", "noise", "amp", "flip", "spread", "spread_t", "expand",
    "lane_sum", "synth", "turn_a", "turn_b", "back_re", "back_im", "gather", "fine_out", "fine_in", "weight",
    "cnt", "msk",
)


def kernel(leg, *refs):
    count = len(OPERANDS)
    sources, out, local = refs[:count], refs[count], refs[count + 1 : 2 * count + 1]
    (
        op_sem,
        lg, wide, ls_x, ls_y, lr_x, lr_y, hg1_x, hg1_y, hg_x, hg_y, hst, accs, fsend, frecv, pt, qt,
        bsend, brecv, psend, precv, coef, gst_x, gst_y, gs1_x, gs1_y, gr1_x, gr1_y, gs2_x, gs2_y, gr2_x, gr2_y,
        digs, dig, thr, own_thr, rows16, h_even, h_odd, hpack, harm_x, harm_y, tot, full_acc,
        lg_sem, ls_sem, lrecv_sem, h1s, h1r, h2s, h2r, fs_sem, fr_sem, bs_sem, br_sem,
        ps_sem, pr_sem, g1s, g1r, g2s, g2r,
    ) = refs[2 * count + 1 :]
    hg1, hg, harm = (hg1_x, hg1_y), (hg_x, hg_y), (harm_x, harm_y)
    gst, gs1, gr1, gs2, gr2 = (gst_x, gst_y), (gs1_x, gs1_y), (gr1_x, gr1_y), (gs2_x, gs2_y), (gr2_x, gr2_y)
    fetches = [
        pltpu.make_async_copy(sources[i], local[i], op_sem.at[i]) for i in range(count)
    ]
    for i in range(7):
        fetches[i].start()
    arrived = set()

    def need(*names):
        for name in names:
            i = OPERANDS.index(name)
            if i not in arrived:
                arrived.add(i)
                fetches[i].wait()

    (
        order, place_, eye, column, noise, amp, flip, spread, spread_t, expand,
        lane_sum, synth, turn_a, turn_b, back_re, back_im, gather, fine_out, fine_in, weight,
        cnt, msk,
    ) = local
    b = lax.axis_index("blk")
    g = lax.axis_index("ma")
    y, x, z = b // 16, (b // 4) % 4, b % 4
    pending = []

    def at(yy, xx, zz, gg):
        return (yy * 16 + xx * 4 + zz, gg)

    def shift(v, d):
        return lax.rem(v + d, 4) if d else v

    def remote(src, dst, ssem, rsem, dev):
        return pltpu.make_async_remote_copy(
            src_ref=src, dst_ref=dst, send_sem=ssem, recv_sem=rsem, device_id=dev, device_id_type=MESH
        )

    def send(src, dst, ssem, rsem, dev):
        c = remote(src, dst, ssem, rsem, dev)
        c.start()
        pending.append(c)

    peers = []
    for dx in range(4):
        for dg in range(4):
            if dx or dg:
                peers.append((0, dx, 0, dg))
    for dy in range(1, 4):
        for dg in range(4):
            peers.append((dy, 0, 0, dg))
    for dy in range(4):
        for dz in range(1, 4):
            peers.append((dy, 0, dz, 0))
    barrier = pltpu.get_barrier_semaphore()
    for dy, dx, dz, dg in peers:
        pl.semaphore_signal(
            barrier, inc=1, device_id=at(shift(y, dy), shift(x, dx), shift(z, dz), shift(g, dg)),
            device_id_type=MESH,
        )

    steps = (1, 3, 2, 0)
    loads = {}
    for d in steps:
        yy = shift(y, d)
        rows = pl.ds(pl.multiple_of(yy * 160, 32), 160)
        for n in range(2):
            c = pltpu.make_async_copy(leg.at[n, rows], lg.at[n, rows], lg_sem.at[n, d])
            c.start()
            loads[d, n] = c

    for i in range(7, count):
        fetches[i].start()
    accs[...] = jnp.zeros_like(accs)
    dig[...] = jnp.zeros_like(dig)
    h_even[...] = jnp.zeros_like(h_even)
    h_odd[...] = jnp.zeros_like(h_odd)
    hpack[...] = jnp.zeros_like(hpack)

    def row_of(rows, i):
        at_row = lax.broadcasted_iota(jnp.int32, rows.shape, 0) == i
        return jnp.sum(jnp.where(at_row, rows, 0.0), axis=0, keepdims=True)

    need("order", "place", "eye", "column")
    slots = order[...].reshape(1, order.shape[0])
    high = (slots >> 6).astype(F32)
    low = (slots & 63).astype(F32)
    for gg in range(4):
        dig[gg : gg + 1, :] = high[:, gg * 640 : gg * 640 + 640]
        dig[8 + gg : 9 + gg, :] = low[:, gg * 640 : gg * 640 + 640]
    placed = nn(dig[...].astype(BF16), place_[...])
    for i in range(16):
        digs[i] = placed[i : i + 1]
    for i in range(8):
        rows16[i : i + 1, :] = digs[g, :, i * 256 : i * 256 + 128]
        rows16[8 + i : 9 + i, :] = digs[g + 8, :, i * 256 : i * 256 + 128]
    lane80 = lax.broadcasted_iota(jnp.int32, (80, 128), 1).astype(F32)
    across16 = nt(eye[...], rows16[...].astype(BF16))
    spreads = nn(across16[0:80].astype(BF16), column[...])
    for i in range(8):
        thr[i // 4, i % 4] = spreads[:, i * 128 : i * 128 + 128] + 128.0 - lane80

    need("noise", "amp", "flip")
    own_thr[...] = jnp.zeros_like(own_thr)
    for k in range(OWN):
        line = row_of(thr[1, y], x * 20 + z * OWN + k)
        own_thr[2 * k : 2 * k + 1, :] = line
        own_thr[2 * k + 1 : 2 * k + 2, :] = line
        h_even[2 * k : 2 * k + 2, :] = noise[2 * k]
        h_odd[2 * k : 2 * k + 2, :] = noise[2 * k + 1]
    own_limit = own_thr[...]
    scale = amp[...].reshape(1, amp.shape[0])

    def where_packed(t):
        m, o = (0, t) if t < XT else (1, t - XT)
        return m, (o // PIECE[m]) * 10, (o % PIECE[m]) * 128

    for t in range(XT + YT):
        m, r0, c0 = where_packed(t)
        value = None
        if t > 0:
            cols = slice((t - 1) * 128, t * 128)
            value = (h_even[:, cols] * scale[:, cols]).astype(BF16).astype(F32)
        if t < XT + YT - 1:
            cols = slice((19 - t) * 128, (20 - t) * 128)
            flipped = nn((h_odd[:, cols] * scale[:, cols]).astype(BF16), flip[128:256, 0:128])
        else:
            flipped = jnp.zeros((16, 128), F32)
        flipped = jnp.where(own_limit >= 128.0 * (t + 1), flipped, 0.0)
        value = flipped if value is None else jnp.where(own_limit <= 128.0 * t, value, flipped)
        hpack[m, r0 : r0 + 10, c0 : c0 + 128] = value[0:10]
    harm[0][...] = hpack[0].astype(BF16)
    harm[1][...] = hpack[1, :, 0:384].astype(BF16)

    def harmonics_copy(stage, m, d, arriving):
        axis = (z, y) if m == 0 else (x, z)
        here = axis[stage]
        there = shift(here, d)
        slot = there if arriving else here
        who = (at(y, x, there, g), at(there, x, z, g)) if m == 0 else (at(y, there, z, g), at(y, x, there, g))
        if stage == 0:
            return remote(harm[m], hg1[m].at[slot], h1s.at[m, d], h1r.at[m, slot], who[0])
        target = hg[0].at[slot] if m == 0 else hg[1].at[:, slot]
        return remote(hg1[m], target, h2s.at[m, d], h2r.at[m, slot], who[1])

    def begin(c):
        c.start()
        pending.append(c)

    def widen(yy):
        rows = pl.ds(pl.multiple_of(yy * 160, 32), 160)

        def body(i, carry):
            n, s = i // 20, i % 20
            block = lg[n, rows, pl.ds(pl.multiple_of(s * 128, 128), 128)].astype(F32)
            wide[n, s, pl.ds(yy * 4, 4)] = block.reshape(4, 40, 128)
            return carry

        lax.fori_loop(0, 40, body, 0, unroll=4)

    def pack(mode, dest):
        buf = (ls_x, ls_y)[mode]
        blocks = [k * 4 + dest if mode == 0 else dest * 4 + k for k in range(4)]
        first, last = (0, XT) if mode == 0 else (XT, XT + YT)

        def one(n, carry):
            def take(s, ab):
                parts = []
                for i in (0, 2):
                    p, q = wide.at[n, s, blocks[i]], wide.at[n, s, blocks[i + 1]]
                    parts.append(p[pl.ds(ab, 16, stride=2), :])
                    parts.append(
                        jnp.concatenate([p[pl.ds(32 + ab, 4, stride=2), :], q[pl.ds(ab, 4, stride=2), :]], axis=0)
                    )
                    parts.append(q[pl.ds(8 + ab, 16, stride=2), :])
                return jnp.concatenate(parts, axis=0)

            pairs = range(first, min(last, 20), 2)
            tall = [
                jnp.concatenate([take(18 - t, 1), take(19 - t, 1)], axis=1).astype(BF16) for t in pairs
            ]
            flipped = nn(jnp.concatenate(tall, axis=0), flip[...])
            limit = thr[mode, dest]
            for t in range(first, last):
                o = (t - first) * 128
                if t < 20:
                    r = ((t - first) // 2) * 80
                    c = ((t - first) % 2) * 128
                    back = flipped[r : r + 80, c : c + 128]
                if t == 0:
                    mix = back
                elif t == 20:
                    mix = take(19, 0)
                else:
                    mix = jnp.where(limit <= 128.0 * t, take(t - 1, 0), back)
                buf[dest, n, :, o : o + 128] = mix.astype(BF16)
            return carry

        lax.fori_loop(0, 2, one, 0)

    send_bufs, recv_bufs = (ls_x, ls_y), (lr_x, lr_y)

    def place(mode, other, r):
        return at(y, other, z, r) if mode == 0 else at(other, x, z, r)

    def mine(mode):
        return x if mode == 0 else y

    def give(mode, d, n):
        dest = shift(mine(mode), d)
        send(
            send_bufs[mode].at[dest, n], recv_bufs[mode].at[mine(mode), n],
            ls_sem.at[mode, d, n], lrecv_sem.at[mode, mine(mode), n], place(mode, dest, g),
        )

    for d in steps:
        for n in range(2):
            loads[d, n].wait()
        widen(shift(y, d))
    pack(0, shift(x, 1))

    pl.semaphore_wait(barrier, len(peers))

    for m in (1, 0):
        for d in (1, 3, 2):
            begin(harmonics_copy(0, m, d, False))
    hg1[0][z] = harm[0][...]
    hg1[1][x] = harm[1][...]
    give(0, 1, 0)
    give(0, 1, 1)
    pack(1, shift(y, 1))
    give(1, 1, 0)
    pack(0, shift(x, 3))
    give(0, 3, 0)
    give(0, 3, 1)
    pack(1, shift(y, 3))
    give(1, 3, 0)
    for m in (0, 1):
        for d in (1, 3, 2):
            harmonics_copy(0, m, d, True).wait_recv()
        for d in (1, 3, 2):
            begin(harmonics_copy(1, m, d, False))
    give(1, 1, 1)
    give(1, 3, 1)
    hg[0][y] = hg1[0][...]
    hg[1][:, z] = hg1[1][...]
    pack(0, shift(x, 2))
    give(0, 2, 0)
    give(0, 2, 1)
    pack(1, shift(y, 2))
    give(1, 2, 0)
    give(1, 2, 1)
    for mode in (1, 0):
        own = mine(mode)
        pack(mode, own)
        recv_bufs[mode][own] = send_bufs[mode][own]

    def digits(i, carry):
        col = pl.ds(pl.multiple_of((i // 4) * 256, 256), 256)
        who = i % 4
        used = (lax.broadcasted_iota(jnp.int32, (1, 256), 1) & 127) < 80
        hi = jnp.where(used, digs[who, :, col], -1.0).astype(jnp.int32)
        lo = digs[who + 8, :, col].astype(jnp.int32)
        pt[i] = jnp.where(
            lax.broadcasted_iota(jnp.int32, (40, 256), 0) == hi, 1.0, 0.0
        ).astype(F32)
        qt[i] = jnp.where(
            (lax.broadcasted_iota(jnp.int32, (128, 256), 0) & 63) == lo, 1.0, 0.0
        ).astype(BF16)
        return carry

    lax.fori_loop(0, 32, digits, 0)

    need("spread_t", "lane_sum")

    def parity(mode):
        line = row_of(rows16[...], 8 + mode * 4 + mine(mode)).astype(jnp.int32)
        return jnp.where((line & 1) == 1, -1.0, 1.0)

    full_acc[...] = jnp.zeros_like(full_acc)
    for m in range(2):
        for dd in (1, 3, 2):
            harmonics_copy(1, m, dd, True).wait_recv()
        width = PIECE[m] * 128
        blocks = hg[m][...].reshape(512, width)

        for c0 in range(0, width, 256):
            c1 = min(width, c0 + 256)
            hst[m, :, c0:c1] = nn(spread_t[...], blocks[:, c0:c1])

    def synthesize(mode, src):
        tiles = (XT, YT)[mode]
        table = recv_bufs[mode]
        own = mine(mode)

        def group(i, carry):
            r0 = pl.multiple_of(i * 16, 16)
            rows = pl.ds(r0, 16)
            limit = thr[mode, own, rows, :]
            total = [[None, None], [None, None]]
            upper = [[None, None], [None, None]]
            for t in range(tiles):
                tile = t + (0 if mode == 0 else XT)
                is_a = limit <= 128 * tile
                for c in range(2):
                    row = pl.ds(pl.multiple_of(((t // PIECE[mode]) * 2 + c) * 80 + r0, 16), 16)
                    h = hst[mode, row, (t % PIECE[mode]) * 128 : (t % PIECE[mode]) * 128 + 128]
                    for n in range(2):
                        v = table[src, n, rows, t * 128 : t * 128 + 128].astype(F32) * h
                        w = jnp.where(is_a, v, 0.0)
                        total[n][c] = v if t == 0 else total[n][c] + v
                        upper[n][c] = w if t == 0 else upper[n][c] + w
            for n in range(2):
                for c in range(2):
                    accs[n, 2 * c, rows, :] = upper[n][c]
                    accs[n, 2 * c + 1, rows, :] = total[n][c] - upper[n][c]
            return carry

        lax.fori_loop(0, 5, group, 0)
        sign = parity(mode)
        signs = jnp.concatenate([sign] * 4, axis=1)
        for n in range(2):
            rows = accs[n].reshape(512, 128)
            hi = rows.astype(BF16)
            lo = (rows - hi.astype(F32)).astype(BF16)
            both = nt(lane_sum[...], jnp.concatenate([hi, lo], axis=1))
            fsend[mode, src, n] = both[0:1]
            fsend[mode, src, n + 2] = both[1:2] * signs

    def scatter(mode, d):
        own = mine(mode)
        p = shift(own, (4 - d) % 4)
        total = full_acc[...]
        for e in range(4):
            r = shift(g, e)
            if d or e:
                remote(
                    fsend.at[mode, p, r], frecv.at[mode, p, r],
                    fs_sem.at[mode, d, e], fr_sem.at[mode, p, r], at(y, x, z, g),
                ).wait_recv()
            i = mode * 16 + p * 4 + r
            row = frecv[mode, p, r]
            digit = pt[i]
            both = jnp.concatenate([digit * row[:, 0:256], digit * row[:, 256:512]], axis=0)
            hi = both.astype(BF16)
            lo = (both - hi.astype(F32)).astype(BF16)
            total = total + nt(jnp.concatenate([hi, lo], axis=0), qt[i])
        full_acc[...] = total

    behind = []
    for d in (0, 3, 1, 2):
        for mode in (1, 0):
            own = mine(mode)
            src = shift(own, d)
            if d:
                for n in range(2):
                    remote(
                        send_bufs[mode].at[src, n], recv_bufs[mode].at[src, n],
                        ls_sem.at[mode, d, n], lrecv_sem.at[mode, src, n], at(y, x, z, g),
                    ).wait_recv()
            synthesize(mode, src)
            for e in range(4):
                r = shift(g, e)
                if d or e:
                    send(
                        fsend.at[mode, src, r], frecv.at[mode, own, g],
                        fs_sem.at[mode, d, e], fr_sem.at[mode, own, g], place(mode, src, r),
                    )
                else:
                    frecv[mode, own, g] = fsend[mode, src, r]
            behind.append((mode, d))
            if len(behind) > 4:
                scatter(*behind.pop(0))
    for mode, d in behind:
        scatter(mode, d)

    need(*OPERANDS)
    h = g % 2

    def halves(v):
        hi = v.astype(BF16)
        return hi, (v - hi.astype(F32)).astype(BF16)

    def thrice(v, axis):
        hi, lo = halves(v)
        return jnp.concatenate([hi, hi, lo], axis=axis)

    full = full_acc[...]
    full = (full[0:80] + full[80:160]) * weight[...]
    section = nn(synth[h], thrice(full, 0))
    turned = section[0:128] * turn_a[h] + section[128:256] * turn_b[h]
    log_density = nt(fine_out[...], thrice(turned, 1))
    inside = msk[...].astype(F32)
    number = inside * cnt[...].astype(F32)
    dens = inside * jnp.exp(log_density)
    psend[0, 0] = jnp.concatenate(
        [jnp.sum(dens, axis=0, keepdims=True), jnp.sum(number, axis=0, keepdims=True)], axis=1
    )
    precv[0, x, g] = psend[0, 0]
    for d in range(4):
        for e in range(4):
            if d or e:
                send(
                    psend.at[0, 0], precv.at[0, x, g], ps_sem.at[0, d, e], pr_sem.at[0, x, g],
                    at(y, shift(x, d), z, shift(g, e)),
                )

    first = nn(fine_in[...], thrice(jnp.concatenate([number, dens], axis=1), 0))
    lines = []
    for f in range(2):
        re, im = first[0:64, f * 128 : f * 128 + 128], first[64:128, f * 128 : f * 128 + 128]
        tre = re * back_re[h] + im * back_im[h]
        tim = im * back_re[h] - re * back_im[h]
        line = thrice(jnp.concatenate([tre, tim], axis=1), 1)
        lines += [line, line]
    modes = nt(gather[h], jnp.concatenate(lines, axis=0))
    modes = jnp.concatenate([modes[:, 0:128] * weight[...], modes[:, 128:256] * weight[...]], axis=0)
    modes_hi = modes.astype(BF16).astype(F32)
    lane = lax.broadcasted_iota(jnp.int32, (160, 128), 1)
    modes = jnp.where(lane < 64, modes_hi, modes - modes_hi).astype(BF16)

    def second_sums():
        for d in range(4):
            for e in range(4):
                if d or e:
                    xx, gg = shift(x, d), shift(g, e)
                    remote(
                        psend.at[0, 0], precv.at[0, xx, gg], ps_sem.at[0, d, e], pr_sem.at[0, xx, gg],
                        at(y, x, z, g),
                    ).wait_recv()
        psend[1, 0] = jnp.sum(precv[0].reshape(16, 1, 256), axis=0)
        precv[1, y, z] = psend[1, 0]
        for d in range(4):
            for e in range(4):
                if d or e:
                    send(
                        psend.at[1, 0], precv.at[1, y, z], ps_sem.at[1, d, e], pr_sem.at[1, y, z],
                        at(shift(y, d), x, shift(z, e), g),
                    )

    for mode in (0, 1):
        own = mine(mode)
        if mode == 1:
            second_sums()
        for d in (2, 1, 3, 0):
            p = shift(own, d)
            for e in range(4):
                gg = shift(g, e)
                i = mode * 16 + p * 4 + gg
                rows = nn(modes, qt[i])
                digit = pt[i]
                for k in range(4):
                    line = jnp.sum(rows[k * 40 : k * 40 + 40] * digit, axis=0, keepdims=True)
                    for ab in range(2):
                        bsend[mode, p, gg, 2 * k + ab : 2 * k + ab + 1, :] = line[:, ab * 128 : ab * 128 + 128]
                if d or e:
                    send(
                        bsend.at[mode, p, gg], brecv.at[mode, own, g],
                        bs_sem.at[mode, d, e], br_sem.at[mode, own, g], place(mode, p, gg),
                    )
                else:
                    brecv[mode, own, g] = bsend[mode, p, gg]

    for d in range(4):
        for e in range(4):
            if d or e:
                yy, zz = shift(y, d), shift(z, e)
                remote(
                    psend.at[1, 0], precv.at[1, yy, zz], ps_sem.at[1, d, e], pr_sem.at[1, yy, zz],
                    at(y, x, z, g),
                ).wait_recv()
    sums = jnp.sum(precv[1].reshape(16, 1, 256), axis=0)
    ratio = jnp.sum(sums[:, 128:256], axis=1, keepdims=True) / jnp.sum(
        sums[:, 0:128], axis=1, keepdims=True
    )

    def analyse(mode):
        tiles = (XT, YT)[mode]
        own = mine(mode)
        for d in range(4):
            for e in range(4):
                if d or e:
                    p, r = shift(own, d), shift(g, e)
                    remote(
                        bsend.at[mode, p, r], brecv.at[mode, p, r],
                        bs_sem.at[mode, d, e], br_sem.at[mode, p, r], at(y, x, z, g),
                    ).wait_recv()
        sign = parity(mode)
        for p in range(4):
            lines = []
            for r in range(4):
                tile = brecv[mode, p, r]
                line = tile - ratio * pltpu.roll(tile, 4, 0)
                line = jnp.where(lax.broadcasted_iota(jnp.int32, (8, 128), 0) < 4, line, 0.0)
                lines.append(line if r < 2 else line * sign)
            across = nt(eye[...], jnp.concatenate(lines, axis=0).astype(BF16))
            coef[p] = nn(across[0:80].astype(BF16), expand[...])
        table = recv_bufs[mode]

        def group(i, carry):
            r0 = pl.multiple_of(i * 16, 16)
            rows = pl.ds(r0, 16)
            limit = thr[mode, own, rows, :]
            for c in range(2):
                co = [
                    [
                        [coef[p, rows, ((n * 2 + c) * 2 + ab) * 128 : ((n * 2 + c) * 2 + ab) * 128 + 128] for ab in range(2)]
                        for n in range(2)
                    ]
                    for p in range(4)
                ]
                for t in range(tiles):
                    is_a = limit <= 128 * (t + (0 if mode == 0 else XT))
                    total = None
                    for p in range(4):
                        for n in range(2):
                            v = table[p, n, rows, t * 128 : t * 128 + 128].astype(F32) * jnp.where(
                                is_a, co[p][n][0], co[p][n][1]
                            )
                            total = v if total is None else total + v
                    row = pl.ds(pl.multiple_of(((t // PIECE[mode]) * 2 + c) * 80 + r0, 16), 16)
                    gst[mode][row, (t % PIECE[mode]) * 128 : (t % PIECE[mode]) * 128 + 128] = total.astype(BF16)
            return carry

        lax.fori_loop(0, 5, group, 0)
        across = y if mode == 0 else x
        for d in (1, 3, 2, 0):
            dest = shift(across, d)
            rows = pl.ds(pl.multiple_of(dest * 128, 128), 128)
            part = nn(spread[rows, :], gst[mode][...]).astype(BF16)
            if d:
                gs1[mode][dest] = part
                who = at(dest, x, z, g) if mode == 0 else at(y, dest, z, g)
                send(
                    gs1[mode].at[dest], gr1[mode].at[across], g1s.at[mode, d], g1r.at[mode, across], who
                )
            else:
                gr1[mode][across] = part

    for mode in (0, 1):
        analyse(mode)

    def sum4(ref):
        total = ref[0].astype(F32)
        for k in range(1, 4):
            total = total + ref[k].astype(F32)
        return total

    for mode in (0, 1):
        across = y if mode == 0 else x
        for d in (1, 3, 2):
            src = shift(across, d)
            remote(
                gs1[mode].at[src], gr1[mode].at[src], g1s.at[mode, d], g1r.at[mode, src], at(y, x, z, g)
            ).wait_recv()
        gs2[mode][...] = sum4(gr1[mode]).astype(BF16).reshape(4, 32, PIECE[mode] * 128)
        gr2[mode][z] = gs2[mode][z]
        for d in (1, 3, 2):
            dest = shift(z, d)
            send(
                gs2[mode].at[dest], gr2[mode].at[z], g2s.at[mode, d], g2r.at[mode, z], at(y, x, dest, g)
            )
    for mode in (1, 0):
        for d in (1, 3, 2):
            src = shift(z, d)
            remote(
                gs2[mode].at[src], gr2[mode].at[src], g2s.at[mode, d], g2r.at[mode, src], at(y, x, z, g)
            ).wait_recv()
        tot[mode, :, 0 : PIECE[mode] * 128] = sum4(gr2[mode])

    own_order = own_limit - 128.0 + lax.broadcasted_iota(jnp.int32, (16, 128), 1).astype(F32)
    lane10 = lax.broadcasted_iota(jnp.int32, (10, 128), 1).astype(F32)
    for t in range(XT + YT):
        m, r0, c0 = where_packed(t)
        value = tot[m, r0 : r0 + 10, c0 : c0 + 128]
        if t > 0:
            cols = slice((t - 1) * 128, t * 128)
            even = jnp.where(own_limit[0:10] <= 128.0 * t, value, 0.0)
            for k in range(OWN):
                out[2 * k, :, cols] = even[2 * k : 2 * k + 2]
        if t < XT + YT - 1:
            s = 19 - t
            cols = slice(s * 128, s * 128 + 128)
            hi = value.astype(BF16)
            lo = (value - hi.astype(F32)).astype(BF16)
            back = nn(hi, flip[128:256, 0:128]) + nn(lo, flip[128:256, 0:128])
            odd = jnp.where(own_order[0:10] + lane10 >= 2559.0 - 128.0 * s, back, 0.0)
            for k in range(OWN):
                out[2 * k + 1, :, cols] = odd[2 * k : 2 * k + 2]

    for c in pending:
        c.wait_send()


def per_device(white_noise, amplitude, legendre, order_of_slot, counts, survey_mask):
    tables = [jnp.asarray(t) for t in selection_tables()]
    operands = (
        [order_of_slot] + tables[:3] + [white_noise, amplitude] + tables[3:]
        + [jnp.asarray(t) for t in dft_tables()]
        + [counts.reshape(64, 128), survey_mask.reshape(64, 128)]
    )
    vmem = pl.BlockSpec(memory_space=pltpu.VMEM)
    dma = pltpu.SemaphoreType.DMA
    got = pl.pallas_call(
        kernel,
        out_shape=jax.ShapeDtypeStruct(white_noise.shape, F32),
        in_specs=[pl.BlockSpec(memory_space=pl.ANY)] * (1 + len(operands)),
        out_specs=vmem,
        scratch_shapes=[pltpu.VMEM(o.shape, o.dtype) for o in operands]
        + [
            dma((len(operands),)),
            pltpu.VMEM((2, 640, 2560), BF16),
            pltpu.VMEM((2, 20, 16, 40, 128), F32),
            pltpu.VMEM((4, 2, 80, LANES[0]), BF16),
            pltpu.VMEM((4, 2, 80, LANES[1]), BF16),
            pltpu.VMEM((4, 2, 80, LANES[0]), BF16),
            pltpu.VMEM((4, 2, 80, LANES[1]), BF16),
            pltpu.VMEM((4, 32, 512), BF16),
            pltpu.VMEM((4, 32, 384), BF16),
            pltpu.VMEM((4, 4, 32, 512), BF16),
            pltpu.VMEM((4, 4, 32, 384), BF16),
            pltpu.VMEM((2, 480, 512), F32),
            pltpu.VMEM((2, 4, 128, 128), F32),
            pltpu.VMEM((2, 4, 4, 1, 512), F32),
            pltpu.VMEM((2, 4, 4, 1, 512), F32),
            pltpu.VMEM((32, 40, 256), F32),
            pltpu.VMEM((32, 128, 256), BF16),
            pltpu.VMEM((2, 4, 4, 8, 128), F32),
            pltpu.VMEM((2, 4, 4, 8, 128), F32),
            pltpu.VMEM((2, 1, 1, 256), F32),
            pltpu.VMEM((2, 4, 4, 1, 256), F32),
            pltpu.VMEM((4, 80, 1024), F32),
            pltpu.VMEM((480, 512), BF16),
            pltpu.VMEM((480, 384), BF16),
            pltpu.VMEM((4, 128, 512), BF16),
            pltpu.VMEM((4, 128, 384), BF16),
            pltpu.VMEM((4, 128, 512), BF16),
            pltpu.VMEM((4, 128, 384), BF16),
            pltpu.VMEM((4, 32, 512), BF16),
            pltpu.VMEM((4, 32, 384), BF16),
            pltpu.VMEM((4, 32, 512), BF16),
            pltpu.VMEM((4, 32, 384), BF16),
            pltpu.VMEM((16, 1, 2048), F32),
            pltpu.VMEM((16, 640), F32),
            pltpu.VMEM((2, 4, 80, 128), F32),
            pltpu.VMEM((16, 128), F32),
            pltpu.VMEM((16, 128), F32),
            pltpu.VMEM((16, 2560), F32),
            pltpu.VMEM((16, 2560), F32),
            pltpu.VMEM((2, 32, 512), F32),
            pltpu.VMEM((32, 512), BF16),
            pltpu.VMEM((32, 384), BF16),
            pltpu.VMEM((2, 32, 512), F32),
            pltpu.VMEM((160, 128), F32),
            dma((2, 4)),
            dma((2, 4, 2)),
            dma((2, 4, 2)),
            dma((2, 4)),
            dma((2, 4)),
            dma((2, 4)),
            dma((2, 4)),
            dma((2, 4, 4)),
            dma((2, 4, 4)),
            dma((2, 4, 4)),
            dma((2, 4, 4)),
            dma((2, 4, 4)),
            dma((2, 4, 4)),
            dma((2, 4)),
            dma((2, 4)),
            dma((2, 4)),
            dma((2, 4)),
        ],
        compiler_params=pltpu.CompilerParams(
            collective_id=0, has_side_effects=True, vmem_limit_bytes=58 * 1024 * 1024
        ),
        name="survey",
    )(legendre, *operands)
    return got * amplitude


def solution(mesh):
    placed = (
        P(("ma", "blk"), None, None),
        P(),
        P("blk", "ma", None),
        P(),
        P(("blk", "ma"), None),
        P(("blk", "ma"), None),
    )
    return jax.shard_map(
        per_device,
        mesh=mesh,
        in_specs=placed,
        out_specs=P(("ma", "blk"), None, None),
        check_vma=False,
    )
```

```python
import functools

import jax
import jax.numpy as jnp
import numpy as np
from jax import lax
from jax.experimental import pallas as pl
from jax.experimental.pallas import tpu as pltpu
from jax.sharding import PartitionSpec as P

MESH = pl.DeviceIdType.MESH
F32 = jnp.float32
BF16 = jnp.bfloat16

SIDE = 4
OWN = 5
PAIRS = 80
XT, YT = 12, 9
PIECE = (XT // 3, YT // 3)
LANES = (XT * 128, YT * 128)


def nt(a, b):
    return lax.dot_general(
        a, b, (((1,), (1,)), ((), ())), preferred_element_type=F32
    )


def nn(a, b):
    return lax.dot_general(
        a, b, (((1,), (0,)), ((), ())), preferred_element_type=F32
    )


def selection_tables():
    flip = np.fliplr(np.eye(256, dtype=np.float32))
    spread = np.zeros((256, 240), np.float32)
    for dev in range(16):
        for j in range(3):
            for k in range(OWN):
                spread[dev * 16 + j * OWN + k, j * 80 + dev * OWN + k] = 1
    alt = np.where(np.arange(128) % 2 == 0, 1.0, -1.0)
    expand = np.zeros((32, 1024), np.float32)
    for r in range(4):
        for e in range(4):
            col = ((r % 2) * 4 + e) * 128
            expand[r * 8 + e, col : col + 128] = 1.0 if r < 2 else alt
    lane_sum = np.zeros((8, 256), np.float32)
    lane_sum[0] = 1
    lane_sum[1] = np.concatenate([alt, alt])
    eye = np.eye(128, dtype=np.float32)
    place = np.zeros((640, 2, 4, 2, 128), np.float32)
    for yy in range(SIDE):
        for xx in range(SIDE):
            for i in range(20):
                for ab in range(2):
                    slot = 2 * (yy * 80 + xx * 20 + i) + ab
                    place[slot, 0, xx, ab, yy * 20 + i] = 1
                    place[slot, 1, yy, ab, xx * 20 + i] = 1
    place = place.reshape(640, 2048)
    column = np.zeros((16, 1024), np.float32)
    for i in range(8):
        column[i, i * 128 : i * 128 + 128] = 64
        column[8 + i, i * 128 : i * 128 + 128] = 1
    return [
        np.asarray(t, jnp.bfloat16)
        for t in (place, eye, column, flip, spread, spread.T.copy(), expand, lane_sum)
    ]


def dft_tables():
    p = np.arange(40)
    q = np.arange(64)
    u = np.arange(64)
    v = np.arange(128)
    synth, turn_a, turn_b, back_re, back_im, gather = [], [], [], [], [], []
    for h in range(2):
        coarse = 2 * np.pi * ((p[:, None] * (2 * v[None, :] + h)) % 256) / 256
        c, s = np.cos(coarse), np.sin(coarse)
        top = np.concatenate([c.T, -s.T], 1)
        low = np.concatenate([s.T, c.T], 1)
        synth.append(np.concatenate([top, low], 0))
        turn = 2 * np.pi * ((q[None, :] * (2 * v[:, None] + h)) % 16384) / 16384
        tc, ts = np.cos(turn), np.sin(turn)
        turn_a.append(np.concatenate([tc, ts], 1))
        turn_b.append(np.concatenate([-ts, tc], 1))
        back_re.append(tc.T.copy())
        back_im.append(ts.T.copy())
        gather.append(
            np.concatenate([np.concatenate([c, s], 1), np.concatenate([-s, c], 1)], 0)
        )
    fine = 2 * np.pi * ((q[None, :] * u[:, None]) % 64) / 64
    fc, fs = np.cos(fine), np.sin(fine)
    fine_out = np.concatenate([fc, -fs], 1)
    fine_in = np.concatenate([fc.T, -fs.T], 0)
    weight = np.full((80, 128), 2.0)
    weight[0, 0] = weight[40, 0] = weight[0, 64] = weight[40, 64] = 1.0

    def split(t):
        t = np.asarray(t, np.float32)
        hi = t.astype(jnp.bfloat16)
        lo = (t - hi.astype(np.float32)).astype(jnp.bfloat16)
        return np.concatenate([hi, lo, hi], axis=-1)

    return [
        split(np.stack(synth)),
        np.stack(turn_a).astype(np.float32),
        np.stack(turn_b).astype(np.float32),
        np.stack(back_re).astype(np.float32),
        np.stack(back_im).astype(np.float32),
        split(np.stack(gather)),
        split(fine_out),
        split(fine_in),
        weight.astype(np.float32),
    ]


OPERANDS = (
    "order", "place", "eye", "column", "noise", "amp", "flip", "spread", "spread_t", "expand",
    "lane_sum", "synth", "turn_a", "turn_b", "back_re", "back_im", "gather", "fine_out", "fine_in", "weight",
    "cnt", "msk",
)


def kernel(leg, *refs):
    count = len(OPERANDS)
    sources, out, local = refs[:count], refs[count], refs[count + 1 : 2 * count + 1]
    (
        op_sem,
        lg, wide, ls_x, ls_y, lr_x, lr_y, hg1_x, hg1_y, hg_x, hg_y, hst, accs, fsend, frecv, pt, qt,
        bsend, brecv, psend, precv, coef, gst_x, gst_y, gs1_x, gs1_y, gr1_x, gr1_y, gs2_x, gs2_y, gr2_x, gr2_y,
        digs, dig, thr, own_thr, rows16, h_even, h_odd, hpack, harm_x, harm_y, tot, full_acc,
        lg_sem, ls_sem, lrecv_sem, h1s, h1r, h2s, h2r, fs_sem, fr_sem, bs_sem, br_sem,
        ps_sem, pr_sem, g1s, g1r, g2s, g2r,
    ) = refs[2 * count + 1 :]
    hg1, hg, harm = (hg1_x, hg1_y), (hg_x, hg_y), (harm_x, harm_y)
    gst, gs1, gr1, gs2, gr2 = (gst_x, gst_y), (gs1_x, gs1_y), (gr1_x, gr1_y), (gs2_x, gs2_y), (gr2_x, gr2_y)
    fetches = [
        pltpu.make_async_copy(sources[i], local[i], op_sem.at[i]) for i in range(count)
    ]
    for i in range(7):
        fetches[i].start()
    arrived = set()

    def need(*names):
        for name in names:
            i = OPERANDS.index(name)
            if i not in arrived:
                arrived.add(i)
                fetches[i].wait()

    (
        order, place_, eye, column, noise, amp, flip, spread, spread_t, expand,
        lane_sum, synth, turn_a, turn_b, back_re, back_im, gather, fine_out, fine_in, weight,
        cnt, msk,
    ) = local
    b = lax.axis_index("blk")
    g = lax.axis_index("ma")
    y, x, z = b // 16, (b // 4) % 4, b % 4
    pending = []

    def at(yy, xx, zz, gg):
        return (yy * 16 + xx * 4 + zz, gg)

    def shift(v, d):
        return lax.rem(v + d, 4) if d else v

    def remote(src, dst, ssem, rsem, dev):
        return pltpu.make_async_remote_copy(
            src_ref=src, dst_ref=dst, send_sem=ssem, recv_sem=rsem, device_id=dev, device_id_type=MESH
        )

    def send(src, dst, ssem, rsem, dev):
        c = remote(src, dst, ssem, rsem, dev)
        c.start()
        pending.append(c)

    peers = []
    for dx in range(4):
        for dg in range(4):
            if dx or dg:
                peers.append((0, dx, 0, dg))
    for dy in range(1, 4):
        for dg in range(4):
            peers.append((dy, 0, 0, dg))
    for dy in range(4):
        for dz in range(1, 4):
            peers.append((dy, 0, dz, 0))
    peers = [q for q in peers if sum(1 for v in q if v) == 1]
    barrier = pltpu.get_barrier_semaphore()
    for dy, dx, dz, dg in peers:
        pl.semaphore_signal(
            barrier, inc=1, device_id=at(shift(y, dy), shift(x, dx), shift(z, dz), shift(g, dg)),
            device_id_type=MESH,
        )

    steps = (1, 3, 2, 0)
    loads = {}
    for d in steps:
        xx = shift(x, d)
        for n in range(2):
            for yy in range(4):
                start = pl.multiple_of(yy * 160 + (xx // 2) * 80 + (xx % 2) * 32, 16)
                c = pltpu.make_async_copy(
                    leg.at[n, pl.ds(start, 48)], lg.at[n, yy, xx], lg_sem.at[d, n, yy]
                )
                c.start()
                loads[d, n, yy] = c

    for i in range(7, count):
        fetches[i].start()
    accs[...] = jnp.zeros_like(accs)
    dig[...] = jnp.zeros_like(dig)
    h_even[...] = jnp.zeros_like(h_even)
    h_odd[...] = jnp.zeros_like(h_odd)
    hpack[...] = jnp.zeros_like(hpack)

    def row_of(rows, i):
        at_row = lax.broadcasted_iota(jnp.int32, rows.shape, 0) == i
        return jnp.sum(jnp.where(at_row, rows, 0.0), axis=0, keepdims=True)

    need("order", "place", "eye", "column")
    slots = order[...].reshape(1, order.shape[0])
    high = (slots >> 6).astype(F32)
    low = (slots & 63).astype(F32)
    for gg in range(4):
        dig[gg : gg + 1, :] = high[:, gg * 640 : gg * 640 + 640]
        dig[8 + gg : 9 + gg, :] = low[:, gg * 640 : gg * 640 + 640]
    placed = nn(dig[...].astype(BF16), place_[...])
    for i in range(16):
        digs[i] = placed[i : i + 1]
    for i in range(8):
        rows16[i : i + 1, :] = digs[g, :, i * 256 : i * 256 + 128]
        rows16[8 + i : 9 + i, :] = digs[g + 8, :, i * 256 : i * 256 + 128]
    lane80 = lax.broadcasted_iota(jnp.int32, (80, 128), 1).astype(F32)
    across16 = nt(eye[...], rows16[...].astype(BF16))
    spreads = nn(across16[0:80].astype(BF16), column[...])
    for i in range(8):
        thr[i // 4, i % 4] = spreads[:, i * 128 : i * 128 + 128] + 128.0 - lane80

    need("noise", "amp", "flip")
    own_thr[...] = jnp.zeros_like(own_thr)
    for k in range(OWN):
        line = row_of(thr[1, y], x * 20 + z * OWN + k)
        for c in range(2):
            own_thr[8 * c + k : 8 * c + k + 1, :] = line
            h_even[8 * c + k : 8 * c + k + 1, :] = noise[2 * k, c : c + 1, :]
            h_odd[8 * c + k : 8 * c + k + 1, :] = noise[2 * k + 1, c : c + 1, :]
    own_limit = own_thr[...]
    scale = amp[...].reshape(1, amp.shape[0])

    def where_packed(t):
        m, o = (0, t) if t < XT else (1, t - XT)
        return m, (o // PIECE[m]) * OWN, (o % PIECE[m]) * 128

    for t in range(XT + YT):
        m, r0, c0 = where_packed(t)
        value = None
        if t > 0:
            cols = slice((t - 1) * 128, t * 128)
            value = (h_even[:, cols] * scale[:, cols]).astype(BF16).astype(F32)
        if t < XT + YT - 1:
            cols = slice((19 - t) * 128, (20 - t) * 128)
            flipped = nn((h_odd[:, cols] * scale[:, cols]).astype(BF16), flip[128:256, 0:128])
        else:
            flipped = jnp.zeros((16, 128), F32)
        flipped = jnp.where(own_limit >= 128.0 * (t + 1), flipped, 0.0)
        value = flipped if value is None else jnp.where(own_limit <= 128.0 * t, value, flipped)
        for c in range(2):
            hpack[m, c * 16 + r0 : c * 16 + r0 + OWN, c0 : c0 + 128] = value[8 * c : 8 * c + OWN]
    harm[0][...] = hpack[0].astype(BF16)
    harm[1][...] = hpack[1, :, 0:384].astype(BF16)

    def harmonics_copy(stage, m, d, arriving):
        axis = (z, y) if m == 0 else (x, z)
        here = axis[stage]
        there = shift(here, d)
        slot = there if arriving else here
        who = (at(y, x, there, g), at(there, x, z, g)) if m == 0 else (at(y, there, z, g), at(y, x, there, g))
        if stage == 0:
            return remote(harm[m], hg1[m].at[slot], h1s.at[m, d], h1r.at[m, slot], who[0])
        target = hg[0].at[slot] if m == 0 else hg[1].at[:, slot]
        return remote(hg1[m], target, h2s.at[m, d], h2r.at[m, slot], who[1])

    def begin(c):
        c.start()
        pending.append(c)

    def widen(d):
        for n in range(2):
            for yy in range(4):
                loads[d, n, yy].wait()
        xx = shift(x, d)
        top = pl.multiple_of(8 - (xx % 2) * 8, 8)

        def body(i, carry):
            n, s = i // 20, i % 20
            for yy in range(4):
                block = lg[n, yy, xx, :, pl.ds(pl.multiple_of(s * 128, 128), 128)]
                wide[n, s, yy * 4 + xx, pl.ds(top, 48), :] = block.astype(F32)
            return carry

        lax.fori_loop(0, 40, body, 0, unroll=2)

    def pack(mode, dest):
        buf = (ls_x, ls_y)[mode]
        blocks = [k * 4 + dest if mode == 0 else dest * 4 + k for k in range(4)]
        first, last = (0, XT) if mode == 0 else (XT, XT + YT)

        def one(n, carry):
            def take(s, ab):
                parts = []
                for i in (0, 2):
                    p, q = wide.at[n, s, blocks[i]], wide.at[n, s, blocks[i + 1]]
                    parts.append(p[pl.ds(8 + ab, 16, stride=2), :])
                    parts.append(
                        jnp.concatenate([p[pl.ds(40 + ab, 4, stride=2), :], q[pl.ds(8 + ab, 4, stride=2), :]], axis=0)
                    )
                    parts.append(q[pl.ds(16 + ab, 16, stride=2), :])
                return jnp.concatenate(parts, axis=0)

            pairs = range(first, min(last, 20), 2)
            tall = [
                jnp.concatenate([take(18 - t, 1), take(19 - t, 1)], axis=1).astype(BF16) for t in pairs
            ]
            flipped = nn(jnp.concatenate(tall, axis=0), flip[...])
            limit = thr[mode, dest]
            for t in range(first, last):
                o = (t - first) * 128
                if t < 20:
                    r = ((t - first) // 2) * 80
                    c = ((t - first) % 2) * 128
                    back = flipped[r : r + 80, c : c + 128]
                if t == 0:
                    mix = back
                elif t == 20:
                    mix = take(19, 0)
                else:
                    mix = jnp.where(limit <= 128.0 * t, take(t - 1, 0), back)
                buf[dest, n, :, o : o + 128] = mix.astype(BF16)
            return carry

        lax.fori_loop(0, 2, one, 0)

    send_bufs, recv_bufs = (ls_x, ls_y), (lr_x, lr_y)

    def place(mode, other, r):
        return at(y, other, z, r) if mode == 0 else at(other, x, z, r)

    def mine(mode):
        return x if mode == 0 else y

    def give(mode, d, n):
        dest = shift(mine(mode), d)
        send(
            send_bufs[mode].at[dest, n], recv_bufs[mode].at[mine(mode), n],
            ls_sem.at[mode, d, n], lrecv_sem.at[mode, mine(mode), n], place(mode, dest, g),
        )

    widen(1)
    pack(0, shift(x, 1))

    pl.semaphore_wait(barrier, len(peers))

    for m in (1, 0):
        for d in (1, 3, 2):
            begin(harmonics_copy(0, m, d, False))
    hg1[0][z] = harm[0][...]
    hg1[1][x] = harm[1][...]
    give(0, 1, 0)
    give(0, 1, 1)
    widen(3)
    pack(0, shift(x, 3))
    give(0, 3, 0)
    give(0, 3, 1)
    widen(2)
    widen(0)
    pack(1, shift(y, 1))
    give(1, 1, 0)
    pack(1, shift(y, 3))
    give(1, 3, 0)
    for m in (0, 1):
        for d in (1, 3, 2):
            harmonics_copy(0, m, d, True).wait_recv()
        for d in (1, 3, 2):
            begin(harmonics_copy(1, m, d, False))
    give(1, 1, 1)
    give(1, 3, 1)
    hg[0][y] = hg1[0][...]
    hg[1][:, z] = hg1[1][...]
    pack(0, shift(x, 2))
    give(0, 2, 0)
    give(0, 2, 1)
    pack(1, shift(y, 2))
    give(1, 2, 0)
    give(1, 2, 1)
    for mode in (1, 0):
        own = mine(mode)
        pack(mode, own)
        recv_bufs[mode][own] = send_bufs[mode][own]

    def digits(i, carry):
        col = pl.ds(pl.multiple_of((i // 4) * 256, 256), 256)
        who = i % 4
        used = (lax.broadcasted_iota(jnp.int32, (1, 256), 1) & 127) < 80
        hi = jnp.where(used, digs[who, :, col], -1.0).astype(jnp.int32)
        lo = digs[who + 8, :, col].astype(jnp.int32)
        pt[i] = jnp.where(
            lax.broadcasted_iota(jnp.int32, (40, 256), 0) == hi, 1.0, 0.0
        ).astype(F32)
        qt[i] = jnp.where(
            (lax.broadcasted_iota(jnp.int32, (128, 256), 0) & 63) == lo, 1.0, 0.0
        ).astype(BF16)
        return carry

    lax.fori_loop(0, 32, digits, 0)

    need("spread_t", "lane_sum")

    def parity(mode):
        line = row_of(rows16[...], 8 + mode * 4 + mine(mode)).astype(jnp.int32)
        return jnp.where((line & 1) == 1, -1.0, 1.0)

    full_acc[...] = jnp.zeros_like(full_acc)
    for m in range(2):
        for dd in (1, 3, 2):
            harmonics_copy(1, m, dd, True).wait_recv()
        width = PIECE[m] * 128
        for c in range(2):
            blocks = hg[m][:, :, c * 16 : c * 16 + 16, :].reshape(256, width)
            for c0 in range(0, width, 256):
                c1 = min(width, c0 + 256)
                hst[m, c * 240 : c * 240 + 240, c0:c1] = nn(spread_t[...], blocks[:, c0:c1])

    def synthesize(mode, src):
        tiles = (XT, YT)[mode]
        table = recv_bufs[mode]
        own = mine(mode)

        def group(i, carry):
            r0 = pl.multiple_of(i * 16, 16)
            rows = pl.ds(r0, 16)
            limit = thr[mode, own, rows, :]
            total = [[None, None], [None, None]]
            upper = [[None, None], [None, None]]
            for t in range(tiles):
                tile = t + (0 if mode == 0 else XT)
                is_a = limit <= 128 * tile
                for c in range(2):
                    row = pl.ds(pl.multiple_of((c * 3 + t // PIECE[mode]) * 80 + r0, 16), 16)
                    h = hst[mode, row, (t % PIECE[mode]) * 128 : (t % PIECE[mode]) * 128 + 128]
                    for n in range(2):
                        v = table[src, n, rows, t * 128 : t * 128 + 128].astype(F32) * h
                        w = jnp.where(is_a, v, 0.0)
                        total[n][c] = v if t == 0 else total[n][c] + v
                        upper[n][c] = w if t == 0 else upper[n][c] + w
            for n in range(2):
                for c in range(2):
                    accs[n, 2 * c, rows, :] = upper[n][c]
                    accs[n, 2 * c + 1, rows, :] = total[n][c] - upper[n][c]
            return carry

        lax.fori_loop(0, 5, group, 0)
        sign = parity(mode)
        signs = jnp.concatenate([sign] * 4, axis=1)
        for n in range(2):
            rows = accs[n].reshape(512, 128)
            hi = rows.astype(BF16)
            lo = (rows - hi.astype(F32)).astype(BF16)
            both = nt(lane_sum[...], jnp.concatenate([hi, lo], axis=1))
            fsend[mode, src, n] = both[0:1]
            fsend[mode, src, n + 2] = both[1:2] * signs

    def scatter(mode, d):
        own = mine(mode)
        p = shift(own, (4 - d) % 4)
        total = full_acc[...]
        for e in range(4):
            r = shift(g, e)
            if d or e:
                remote(
                    fsend.at[mode, p, r], frecv.at[mode, p, r],
                    fs_sem.at[mode, d, e], fr_sem.at[mode, p, r], at(y, x, z, g),
                ).wait_recv()
            i = mode * 16 + p * 4 + r
            row = frecv[mode, p, r]
            digit = pt[i]
            both = jnp.concatenate([digit * row[:, 0:256], digit * row[:, 256:512]], axis=0)
            hi = both.astype(BF16)
            lo = (both - hi.astype(F32)).astype(BF16)
            total = total + nt(jnp.concatenate([hi, lo], axis=0), qt[i])
        full_acc[...] = total

    behind = []
    for d in (0, 3, 1, 2):
        for mode in (1, 0):
            own = mine(mode)
            src = shift(own, d)
            if d:
                for n in range(2):
                    remote(
                        send_bufs[mode].at[src, n], recv_bufs[mode].at[src, n],
                        ls_sem.at[mode, d, n], lrecv_sem.at[mode, src, n], at(y, x, z, g),
                    ).wait_recv()
            synthesize(mode, src)
            for e in range(4):
                r = shift(g, e)
                if d or e:
                    send(
                        fsend.at[mode, src, r], frecv.at[mode, own, g],
                        fs_sem.at[mode, d, e], fr_sem.at[mode, own, g], place(mode, src, r),
                    )
                else:
                    frecv[mode, own, g] = fsend[mode, src, r]
            behind.append((mode, d))
            if len(behind) > 4:
                scatter(*behind.pop(0))
    for mode, d in behind:
        scatter(mode, d)

    need(*OPERANDS)
    h = g % 2

    def halves(v):
        hi = v.astype(BF16)
        return hi, (v - hi.astype(F32)).astype(BF16)

    def thrice(v, axis):
        hi, lo = halves(v)
        return jnp.concatenate([hi, hi, lo], axis=axis)

    full = full_acc[...]
    full = (full[0:80] + full[80:160]) * weight[...]
    section = nn(synth[h], thrice(full, 0))
    turned = section[0:128] * turn_a[h] + section[128:256] * turn_b[h]
    log_density = nt(fine_out[...], thrice(turned, 1))
    inside = msk[...].astype(F32)
    number = inside * cnt[...].astype(F32)
    dens = inside * jnp.exp(log_density)
    psend[0, 0] = jnp.concatenate(
        [jnp.sum(dens, axis=0, keepdims=True), jnp.sum(number, axis=0, keepdims=True)], axis=1
    )
    precv[0, x, g] = psend[0, 0]
    for d in range(4):
        for e in range(4):
            if d or e:
                send(
                    psend.at[0, 0], precv.at[0, x, g], ps_sem.at[0, d, e], pr_sem.at[0, x, g],
                    at(y, shift(x, d), z, shift(g, e)),
                )

    first = nn(fine_in[...], thrice(jnp.concatenate([number, dens], axis=1), 0))
    lines = []
    for f in range(2):
        re, im = first[0:64, f * 128 : f * 128 + 128], first[64:128, f * 128 : f * 128 + 128]
        tre = re * back_re[h] + im * back_im[h]
        tim = im * back_re[h] - re * back_im[h]
        line = thrice(jnp.concatenate([tre, tim], axis=1), 1)
        lines += [line, line]
    modes = nt(gather[h], jnp.concatenate(lines, axis=0))
    modes = jnp.concatenate([modes[:, 0:128] * weight[...], modes[:, 128:256] * weight[...]], axis=0)
    modes_hi = modes.astype(BF16).astype(F32)
    lane = lax.broadcasted_iota(jnp.int32, (160, 128), 1)
    modes = jnp.where(lane < 64, modes_hi, modes - modes_hi).astype(BF16)

    def second_sums():
        for d in range(4):
            for e in range(4):
                if d or e:
                    xx, gg = shift(x, d), shift(g, e)
                    remote(
                        psend.at[0, 0], precv.at[0, xx, gg], ps_sem.at[0, d, e], pr_sem.at[0, xx, gg],
                        at(y, x, z, g),
                    ).wait_recv()
        psend[1, 0] = jnp.sum(precv[0].reshape(16, 1, 256), axis=0)
        precv[1, y, z] = psend[1, 0]
        for d in range(4):
            for e in range(4):
                if d or e:
                    send(
                        psend.at[1, 0], precv.at[1, y, z], ps_sem.at[1, d, e], pr_sem.at[1, y, z],
                        at(shift(y, d), x, shift(z, e), g),
                    )

    for mode in (0, 1):
        own = mine(mode)
        if mode == 1:
            second_sums()
        for d in (2, 1, 3, 0):
            p = shift(own, d)
            for e in range(4):
                gg = shift(g, e)
                i = mode * 16 + p * 4 + gg
                rows = nn(modes, qt[i])
                digit = pt[i]
                for k in range(4):
                    line = jnp.sum(rows[k * 40 : k * 40 + 40] * digit, axis=0, keepdims=True)
                    for ab in range(2):
                        bsend[mode, p, gg, 2 * k + ab : 2 * k + ab + 1, :] = line[:, ab * 128 : ab * 128 + 128]
                if d or e:
                    send(
                        bsend.at[mode, p, gg], brecv.at[mode, own, g],
                        bs_sem.at[mode, d, e], br_sem.at[mode, own, g], place(mode, p, gg),
                    )
                else:
                    brecv[mode, own, g] = bsend[mode, p, gg]

    for d in range(4):
        for e in range(4):
            if d or e:
                yy, zz = shift(y, d), shift(z, e)
                remote(
                    psend.at[1, 0], precv.at[1, yy, zz], ps_sem.at[1, d, e], pr_sem.at[1, yy, zz],
                    at(y, x, z, g),
                ).wait_recv()
    sums = jnp.sum(precv[1].reshape(16, 1, 256), axis=0)
    ratio = jnp.sum(sums[:, 128:256], axis=1, keepdims=True) / jnp.sum(
        sums[:, 0:128], axis=1, keepdims=True
    )

    def coefficients(mode):
        own = mine(mode)
        for d in range(4):
            for e in range(4):
                if d or e:
                    p, r = shift(own, d), shift(g, e)
                    remote(
                        bsend.at[mode, p, r], brecv.at[mode, p, r],
                        bs_sem.at[mode, d, e], br_sem.at[mode, p, r], at(y, x, z, g),
                    ).wait_recv()
        sign = parity(mode)
        for p in range(4):
            lines = []
            for r in range(4):
                tile = brecv[mode, p, r]
                line = tile - ratio * pltpu.roll(tile, 4, 0)
                line = jnp.where(lax.broadcasted_iota(jnp.int32, (8, 128), 0) < 4, line, 0.0)
                lines.append(line if r < 2 else line * sign)
            across = nt(eye[...], jnp.concatenate(lines, axis=0).astype(BF16))
            coef[mode, p] = nn(across[0:80].astype(BF16), expand[...])

    def analyse(mode, c):
        tiles = (XT, YT)[mode]
        own = mine(mode)
        table = recv_bufs[mode]

        def group(i, carry):
            r0 = pl.multiple_of(i * 16, 16)
            rows = pl.ds(r0, 16)
            limit = thr[mode, own, rows, :]
            co = []
            for p in range(4):
                for n in range(2):
                    at_lane = ((n * 2 + c) * 2) * 128
                    co.append(
                        (
                            coef[mode, p, rows, at_lane : at_lane + 128],
                            coef[mode, p, rows, at_lane + 128 : at_lane + 256],
                        )
                    )
            for t in range(tiles):
                is_a = limit <= 128.0 * (t + (0 if mode == 0 else XT))
                total = None
                for p in range(4):
                    for n in range(2):
                        v = table[p, n, rows, t * 128 : t * 128 + 128].astype(F32) * jnp.where(
                            is_a, co[2 * p + n][0], co[2 * p + n][1]
                        )
                        total = v if total is None else total + v
                row = pl.ds(pl.multiple_of((c * 3 + t // PIECE[mode]) * 80 + r0, 16), 16)
                at_lane = (t % PIECE[mode]) * 128
                gst[mode][row, at_lane : at_lane + 128] = total.astype(BF16)
            return carry

        lax.fori_loop(0, 5, group, 0)
        across = y if mode == 0 else x
        for d in (1, 3, 2, 0):
            dest = shift(across, d)
            rows = pl.ds(pl.multiple_of(dest * 64, 64), 64)
            part = nn(spread[rows, :], gst[mode][c * 240 : c * 240 + 240, :]).astype(BF16)
            if d:
                gs1[mode][c, dest] = part
                begin(first_sum(mode, c, d, False))
            else:
                gr1[mode][c, across] = part

    def first_sum(mode, c, d, arriving):
        across = y if mode == 0 else x
        there = shift(across, d)
        slot = there if arriving else across
        who = at(there, x, z, g) if mode == 0 else at(y, there, z, g)
        return remote(
            gs1[mode].at[c, there], gr1[mode].at[c, slot], g1s.at[mode, c, d], g1r.at[mode, c, slot], who
        )

    def second_sum(mode, c, d, arriving):
        there = shift(z, d)
        slot = there if arriving else z
        return remote(
            gs2[mode].at[c, there], gr2[mode].at[c, slot], g2s.at[mode, c, d], g2r.at[mode, c, slot],
            at(y, x, there, g),
        )

    def sum4(ref, c):
        total = ref[c, 0].astype(F32)
        for k in range(1, 4):
            total = total + ref[c, k].astype(F32)
        return total

    for mode, c in ((0, 0), (1, 0), (0, 1), (1, 1)):
        if c == 0:
            coefficients(mode)
        analyse(mode, c)

    for mode, c in ((0, 0), (1, 0), (0, 1), (1, 1)):
        for d in (1, 3, 2):
            first_sum(mode, c, d, True).wait_recv()
        gs2[mode][c] = sum4(gr1[mode], c).astype(BF16).reshape(4, 16, PIECE[mode] * 128)
        for d in (2, 1, 3):
            begin(second_sum(mode, c, d, False))
        gr2[mode][c, z] = gs2[mode][c, z]
    tot[...] = jnp.zeros_like(tot)
    for mode, c in ((0, 0), (1, 0), (0, 1), (1, 1)):
        for d in (1, 3, 2):
            second_sum(mode, c, d, True).wait_recv()
        tot[mode, c * 16 : c * 16 + 16, 0 : PIECE[mode] * 128] = sum4(gr2[mode], c)

    own_order = own_limit - 128.0 + lax.broadcasted_iota(jnp.int32, (16, 128), 1).astype(F32)
    lane16 = lax.broadcasted_iota(jnp.int32, (16, 128), 1).astype(F32)
    for t in range(XT + YT):
        m, r0, c0 = where_packed(t)
        value = jnp.concatenate(
            [tot[m, c * 16 + r0 : c * 16 + r0 + 8, c0 : c0 + 128] for c in range(2)], axis=0
        )
        if t > 0:
            cols = slice((t - 1) * 128, t * 128)
            even = jnp.where(own_limit <= 128.0 * t, value, 0.0)
            for k in range(OWN):
                for c in range(2):
                    out[2 * k, c : c + 1, cols] = even[8 * c + k : 8 * c + k + 1]
        if t < XT + YT - 1:
            s = 19 - t
            cols = slice(s * 128, s * 128 + 128)
            hi = value.astype(BF16)
            lo = (value - hi.astype(F32)).astype(BF16)
            back = nn(hi, flip[128:256, 0:128]) + nn(lo, flip[128:256, 0:128])
            odd = jnp.where(own_order + lane16 >= 2559.0 - 128.0 * s, back, 0.0)
            for k in range(OWN):
                for c in range(2):
                    out[2 * k + 1, c : c + 1, cols] = odd[8 * c + k : 8 * c + k + 1]

    for c in pending:
        c.wait_send()


def per_device(white_noise, amplitude, legendre, order_of_slot, counts, survey_mask):
    tables = [jnp.asarray(t) for t in selection_tables()]
    operands = (
        [order_of_slot] + tables[:3] + [white_noise, amplitude] + tables[3:]
        + [jnp.asarray(t) for t in dft_tables()]
        + [counts.reshape(64, 128), survey_mask.reshape(64, 128)]
    )
    vmem = pl.BlockSpec(memory_space=pltpu.VMEM)
    dma = pltpu.SemaphoreType.DMA
    got = pl.pallas_call(
        kernel,
        out_shape=jax.ShapeDtypeStruct(white_noise.shape, F32),
        in_specs=[pl.BlockSpec(memory_space=pl.ANY)] * (1 + len(operands)),
        out_specs=vmem,
        scratch_shapes=[pltpu.VMEM(o.shape, o.dtype) for o in operands]
        + [
            dma((len(operands),)),
            pltpu.VMEM((2, 4, 4, 48, 2560), BF16),
            pltpu.VMEM((2, 20, 16, 56, 128), F32),
            pltpu.VMEM((4, 2, 80, LANES[0]), BF16),
            pltpu.VMEM((4, 2, 80, LANES[1]), BF16),
            pltpu.VMEM((4, 2, 80, LANES[0]), BF16),
            pltpu.VMEM((4, 2, 80, LANES[1]), BF16),
            pltpu.VMEM((4, 32, 512), BF16),
            pltpu.VMEM((4, 32, 384), BF16),
            pltpu.VMEM((4, 4, 32, 512), BF16),
            pltpu.VMEM((4, 4, 32, 384), BF16),
            pltpu.VMEM((2, 480, 512), F32),
            pltpu.VMEM((2, 4, 128, 128), F32),
            pltpu.VMEM((2, 4, 4, 1, 512), F32),
            pltpu.VMEM((2, 4, 4, 1, 512), F32),
            pltpu.VMEM((32, 40, 256), F32),
            pltpu.VMEM((32, 128, 256), BF16),
            pltpu.VMEM((2, 4, 4, 8, 128), F32),
            pltpu.VMEM((2, 4, 4, 8, 128), F32),
            pltpu.VMEM((2, 1, 1, 256), F32),
            pltpu.VMEM((2, 4, 4, 1, 256), F32),
            pltpu.VMEM((2, 4, 80, 1024), F32),
            pltpu.VMEM((480, 512), BF16),
            pltpu.VMEM((480, 384), BF16),
            pltpu.VMEM((2, 4, 64, 512), BF16),
            pltpu.VMEM((2, 4, 64, 384), BF16),
            pltpu.VMEM((2, 4, 64, 512), BF16),
            pltpu.VMEM((2, 4, 64, 384), BF16),
            pltpu.VMEM((2, 4, 16, 512), BF16),
            pltpu.VMEM((2, 4, 16, 384), BF16),
            pltpu.VMEM((2, 4, 16, 512), BF16),
            pltpu.VMEM((2, 4, 16, 384), BF16),
            pltpu.VMEM((16, 1, 2048), F32),
            pltpu.VMEM((16, 640), F32),
            pltpu.VMEM((2, 4, 80, 128), F32),
            pltpu.VMEM((16, 128), F32),
            pltpu.VMEM((16, 128), F32),
            pltpu.VMEM((16, 2560), F32),
            pltpu.VMEM((16, 2560), F32),
            pltpu.VMEM((2, 32, 512), F32),
            pltpu.VMEM((32, 512), BF16),
            pltpu.VMEM((32, 384), BF16),
            pltpu.VMEM((2, 40, 512), F32),
            pltpu.VMEM((160, 128), F32),
            dma((4, 2, 4)),
            dma((2, 4, 2)),
            dma((2, 4, 2)),
            dma((2, 4)),
            dma((2, 4)),
            dma((2, 4)),
            dma((2, 4)),
            dma((2, 4, 4)),
            dma((2, 4, 4)),
            dma((2, 4, 4)),
            dma((2, 4, 4)),
            dma((2, 4, 4)),
            dma((2, 4, 4)),
            dma((2, 2, 4)),
            dma((2, 2, 4)),
            dma((2, 2, 4)),
            dma((2, 2, 4)),
        ],
        compiler_params=pltpu.CompilerParams(
            collective_id=0, has_side_effects=True, vmem_limit_bytes=58 * 1024 * 1024
        ),
        name="survey",
    )(legendre, *operands)
    return got * amplitude


def solution(mesh):
    placed = (
        P(("ma", "blk"), None, None),
        P(),
        P("blk", "ma", None),
        P(),
        P(("blk", "ma"), None),
        P(("blk", "ma"), None),
    )
    return jax.shard_map(
        per_device,
        mesh=mesh,
        in_specs=placed,
        out_specs=P(("ma", "blk"), None, None),
        check_vma=False,
    )
```

```python
import functools

import jax
import jax.numpy as jnp
import numpy as np
from jax import lax
from jax.experimental import pallas as pl
from jax.experimental.pallas import tpu as pltpu
from jax.sharding import PartitionSpec as P

MESH = pl.DeviceIdType.MESH
F32 = jnp.float32
BF16 = jnp.bfloat16

SIDE = 4
OWN = 5
PAIRS = 80
XT, YT = 12, 9
PIECE = (XT // 3, YT // 3)
LANES = (XT * 128, YT * 128)


def nt(a, b):
    return lax.dot_general(
        a, b, (((1,), (1,)), ((), ())), preferred_element_type=F32
    )


def nn(a, b):
    return lax.dot_general(
        a, b, (((1,), (0,)), ((), ())), preferred_element_type=F32
    )


def selection_tables():
    flip = np.fliplr(np.eye(256, dtype=np.float32))
    spread = np.zeros((256, 240), np.float32)
    for dev in range(16):
        for j in range(3):
            for k in range(OWN):
                spread[dev * 16 + j * OWN + k, j * 80 + dev * OWN + k] = 1
    alt = np.where(np.arange(128) % 2 == 0, 1.0, -1.0)
    expand = np.zeros((32, 1024), np.float32)
    for r in range(4):
        for e in range(4):
            col = ((r % 2) * 4 + e) * 128
            expand[r * 8 + e, col : col + 128] = 1.0 if r < 2 else alt
    lane_sum = np.zeros((8, 256), np.float32)
    lane_sum[0] = 1
    lane_sum[1] = np.concatenate([alt, alt])
    eye = np.eye(128, dtype=np.float32)
    place = np.zeros((640, 2, 4, 2, 128), np.float32)
    for yy in range(SIDE):
        for xx in range(SIDE):
            for i in range(20):
                for ab in range(2):
                    slot = 2 * (yy * 80 + xx * 20 + i) + ab
                    place[slot, 0, xx, ab, yy * 20 + i] = 1
                    place[slot, 1, yy, ab, xx * 20 + i] = 1
    place = place.reshape(640, 2048)
    column = np.zeros((16, 1024), np.float32)
    for i in range(8):
        column[i, i * 128 : i * 128 + 128] = 64
        column[8 + i, i * 128 : i * 128 + 128] = 1
    return [
        np.asarray(t, jnp.bfloat16)
        for t in (place, eye, column, flip, spread, spread.T.copy(), expand, lane_sum)
    ]


def dft_tables():
    p = np.arange(40)
    q = np.arange(64)
    u = np.arange(64)
    v = np.arange(128)
    synth, turn_a, turn_b, back_re, back_im, gather = [], [], [], [], [], []
    for h in range(2):
        coarse = 2 * np.pi * ((p[:, None] * (2 * v[None, :] + h)) % 256) / 256
        c, s = np.cos(coarse), np.sin(coarse)
        top = np.concatenate([c.T, -s.T], 1)
        low = np.concatenate([s.T, c.T], 1)
        synth.append(np.concatenate([top, low], 0))
        turn = 2 * np.pi * ((q[None, :] * (2 * v[:, None] + h)) % 16384) / 16384
        tc, ts = np.cos(turn), np.sin(turn)
        turn_a.append(np.concatenate([tc, ts], 1))
        turn_b.append(np.concatenate([-ts, tc], 1))
        back_re.append(tc.T.copy())
        back_im.append(ts.T.copy())
        gather.append(
            np.concatenate([np.concatenate([c, s], 1), np.concatenate([-s, c], 1)], 0)
        )
    fine = 2 * np.pi * ((q[None, :] * u[:, None]) % 64) / 64
    fc, fs = np.cos(fine), np.sin(fine)
    fine_out = np.concatenate([fc, -fs], 1)
    fine_in = np.concatenate([fc.T, -fs.T], 0)
    weight = np.full((80, 128), 2.0)
    weight[0, 0] = weight[40, 0] = weight[0, 64] = weight[40, 64] = 1.0

    def split(t):
        t = np.asarray(t, np.float32)
        hi = t.astype(jnp.bfloat16)
        lo = (t - hi.astype(np.float32)).astype(jnp.bfloat16)
        return np.concatenate([hi, lo, hi], axis=-1)

    return [
        split(np.stack(synth)),
        np.stack(turn_a).astype(np.float32),
        np.stack(turn_b).astype(np.float32),
        np.stack(back_re).astype(np.float32),
        np.stack(back_im).astype(np.float32),
        split(np.stack(gather)),
        split(fine_out),
        split(fine_in),
        weight.astype(np.float32),
    ]


OPERANDS = (
    "order", "place", "eye", "column", "noise", "amp", "flip", "spread", "spread_t", "expand",
    "lane_sum", "synth", "turn_a", "turn_b", "back_re", "back_im", "gather", "fine_out", "fine_in", "weight",
    "cnt", "msk",
)


def kernel(leg, *refs):
    count = len(OPERANDS)
    sources, out, local = refs[:count], refs[count], refs[count + 1 : 2 * count + 1]
    (
        op_sem,
        lg, wide, ls_x, ls_y, lr_x, lr_y, hg1_x, hg1_y, hg_x, hg_y, hst, accs, fsend, frecv, pt, qt,
        bsend, brecv, psend, precv, coef, gst_x, gst_y, gs1_x, gs1_y, gr1_x, gr1_y, gs2_x, gs2_y, gr2_x, gr2_y,
        digs, dig, thr, own_thr, rows16, h_even, h_odd, hpack, harm_x, harm_y, tot, full_acc,
        lg_sem, ls_sem, lrecv_sem, h1s, h1r, h2s, h2r, fs_sem, fr_sem, bs_sem, br_sem,
        ps_sem, pr_sem, g1s, g1r, g2s, g2r,
    ) = refs[2 * count + 1 :]
    hg1, hg, harm = (hg1_x, hg1_y), (hg_x, hg_y), (harm_x, harm_y)
    gst, gs1, gr1, gs2, gr2 = (gst_x, gst_y), (gs1_x, gs1_y), (gr1_x, gr1_y), (gs2_x, gs2_y), (gr2_x, gr2_y)
    fetches = [
        pltpu.make_async_copy(sources[i], local[i], op_sem.at[i]) for i in range(count)
    ]
    for i in range(7):
        fetches[i].start()
    arrived = set()

    def need(*names):
        for name in names:
            i = OPERANDS.index(name)
            if i not in arrived:
                arrived.add(i)
                fetches[i].wait()

    (
        order, place_, eye, column, noise, amp, flip, spread, spread_t, expand,
        lane_sum, synth, turn_a, turn_b, back_re, back_im, gather, fine_out, fine_in, weight,
        cnt, msk,
    ) = local
    b = lax.axis_index("blk")
    g = lax.axis_index("ma")
    y, x, z = b // 16, (b // 4) % 4, b % 4
    pending = []

    def at(yy, xx, zz, gg):
        return (yy * 16 + xx * 4 + zz, gg)

    def shift(v, d):
        return lax.rem(v + d, 4) if d else v

    def remote(src, dst, ssem, rsem, dev):
        return pltpu.make_async_remote_copy(
            src_ref=src, dst_ref=dst, send_sem=ssem, recv_sem=rsem, device_id=dev, device_id_type=MESH
        )

    def send(src, dst, ssem, rsem, dev):
        c = remote(src, dst, ssem, rsem, dev)
        c.start()
        pending.append(c)

    peers = []
    for dx in range(4):
        for dg in range(4):
            if dx or dg:
                peers.append((0, dx, 0, dg))
    for dy in range(1, 4):
        for dg in range(4):
            peers.append((dy, 0, 0, dg))
    for dy in range(4):
        for dz in range(1, 4):
            peers.append((dy, 0, dz, 0))
    peers = [q for q in peers if sum(1 for v in q if v) == 1]
    barrier = pltpu.get_barrier_semaphore()
    for dy, dx, dz, dg in peers:
        pl.semaphore_signal(
            barrier, inc=1, device_id=at(shift(y, dy), shift(x, dx), shift(z, dz), shift(g, dg)),
            device_id_type=MESH,
        )

    steps = (1, 3, 2, 0)
    loads = {}
    for d in steps:
        xx = shift(x, d)
        for n in range(2):
            for yy in range(4):
                start = pl.multiple_of(yy * 160 + (xx // 2) * 80 + (xx % 2) * 32, 16)
                c = pltpu.make_async_copy(
                    leg.at[n, pl.ds(start, 48)], lg.at[n, yy, xx], lg_sem.at[d, n, yy]
                )
                c.start()
                loads[d, n, yy] = c

    for i in range(7, count):
        fetches[i].start()
    accs[...] = jnp.zeros_like(accs)
    dig[...] = jnp.zeros_like(dig)
    h_even[...] = jnp.zeros_like(h_even)
    h_odd[...] = jnp.zeros_like(h_odd)
    hpack[...] = jnp.zeros_like(hpack)

    def row_of(rows, i):
        at_row = lax.broadcasted_iota(jnp.int32, rows.shape, 0) == i
        return jnp.sum(jnp.where(at_row, rows, 0.0), axis=0, keepdims=True)

    need("order", "place", "eye", "column")
    slots = order[...].reshape(1, order.shape[0])
    high = (slots >> 6).astype(F32)
    low = (slots & 63).astype(F32)
    for gg in range(4):
        dig[gg : gg + 1, :] = high[:, gg * 640 : gg * 640 + 640]
        dig[8 + gg : 9 + gg, :] = low[:, gg * 640 : gg * 640 + 640]
    placed = nn(dig[...].astype(BF16), place_[...])
    for i in range(16):
        digs[i] = placed[i : i + 1]
    for i in range(8):
        rows16[i : i + 1, :] = digs[g, :, i * 256 : i * 256 + 128]
        rows16[8 + i : 9 + i, :] = digs[g + 8, :, i * 256 : i * 256 + 128]
    lane80 = lax.broadcasted_iota(jnp.int32, (80, 128), 1).astype(F32)
    across16 = nt(eye[...], rows16[...].astype(BF16))
    spreads = nn(across16[0:80].astype(BF16), column[...])
    for i in range(8):
        thr[i // 4, i % 4] = spreads[:, i * 128 : i * 128 + 128] + 128.0 - lane80

    need("noise", "amp", "flip")
    own_thr[...] = jnp.zeros_like(own_thr)
    for k in range(OWN):
        line = row_of(thr[1, y], x * 20 + z * OWN + k)
        for c in range(2):
            own_thr[8 * c + k : 8 * c + k + 1, :] = line
            h_even[8 * c + k : 8 * c + k + 1, :] = noise[2 * k, c : c + 1, :]
            h_odd[8 * c + k : 8 * c + k + 1, :] = noise[2 * k + 1, c : c + 1, :]
    own_limit = own_thr[...]
    scale = amp[...].reshape(1, amp.shape[0])

    def where_packed(t):
        m, o = (0, t) if t < XT else (1, t - XT)
        return m, (o // PIECE[m]) * OWN, (o % PIECE[m]) * 128

    for t in range(XT + YT):
        m, r0, c0 = where_packed(t)
        value = None
        if t > 0:
            cols = slice((t - 1) * 128, t * 128)
            value = (h_even[:, cols] * scale[:, cols]).astype(BF16).astype(F32)
        if t < XT + YT - 1:
            cols = slice((19 - t) * 128, (20 - t) * 128)
            flipped = nn((h_odd[:, cols] * scale[:, cols]).astype(BF16), flip[128:256, 0:128])
        else:
            flipped = jnp.zeros((16, 128), F32)
        flipped = jnp.where(own_limit >= 128.0 * (t + 1), flipped, 0.0)
        value = flipped if value is None else jnp.where(own_limit <= 128.0 * t, value, flipped)
        for c in range(2):
            hpack[m, c * 16 + r0 : c * 16 + r0 + OWN, c0 : c0 + 128] = value[8 * c : 8 * c + OWN]
    harm[0][...] = hpack[0].astype(BF16)
    harm[1][...] = hpack[1, :, 0:384].astype(BF16)

    def harmonics_copy(stage, m, d, arriving):
        axis = (z, y) if m == 0 else (x, z)
        here = axis[stage]
        there = shift(here, d)
        slot = there if arriving else here
        who = (at(y, x, there, g), at(there, x, z, g)) if m == 0 else (at(y, there, z, g), at(y, x, there, g))
        if stage == 0:
            return remote(harm[m], hg1[m].at[slot], h1s.at[m, d], h1r.at[m, slot], who[0])
        target = hg[0].at[slot] if m == 0 else hg[1].at[:, slot]
        return remote(hg1[m], target, h2s.at[m, d], h2r.at[m, slot], who[1])

    def begin(c):
        c.start()
        pending.append(c)

    def widen(d):
        for n in range(2):
            for yy in range(4):
                loads[d, n, yy].wait()
        xx = shift(x, d)
        top = pl.multiple_of(8 - (xx % 2) * 8, 8)

        def body(i, carry):
            n, s = i // 20, i % 20
            for yy in range(4):
                block = lg[n, yy, xx, :, pl.ds(pl.multiple_of(s * 128, 128), 128)]
                wide[n, s, yy * 4 + xx, pl.ds(top, 48), :] = block.astype(F32)
            return carry

        lax.fori_loop(0, 40, body, 0, unroll=2)

    def pack(mode, dest):
        buf = (ls_x, ls_y)[mode]
        blocks = [k * 4 + dest if mode == 0 else dest * 4 + k for k in range(4)]
        first, last = (0, XT) if mode == 0 else (XT, XT + YT)

        def one(n, carry):
            def take(s, ab):
                parts = []
                for i in (0, 2):
                    p, q = wide.at[n, s, blocks[i]], wide.at[n, s, blocks[i + 1]]
                    parts.append(p[pl.ds(8 + ab, 16, stride=2), :])
                    parts.append(
                        jnp.concatenate([p[pl.ds(40 + ab, 4, stride=2), :], q[pl.ds(8 + ab, 4, stride=2), :]], axis=0)
                    )
                    parts.append(q[pl.ds(16 + ab, 16, stride=2), :])
                return jnp.concatenate(parts, axis=0)

            pairs = range(first, min(last, 20), 2)
            tall = [
                jnp.concatenate([take(18 - t, 1), take(19 - t, 1)], axis=1).astype(BF16) for t in pairs
            ]
            flipped = nn(jnp.concatenate(tall, axis=0), flip[...])
            limit = thr[mode, dest]
            for t in range(first, last):
                o = (t - first) * 128
                if t < 20:
                    r = ((t - first) // 2) * 80
                    c = ((t - first) % 2) * 128
                    back = flipped[r : r + 80, c : c + 128]
                if t == 0:
                    mix = back
                elif t == 20:
                    mix = take(19, 0)
                else:
                    mix = jnp.where(limit <= 128.0 * t, take(t - 1, 0), back)
                buf[dest, n, :, o : o + 128] = mix.astype(BF16)
            return carry

        lax.fori_loop(0, 2, one, 0)

    send_bufs, recv_bufs = (ls_x, ls_y), (lr_x, lr_y)

    def place(mode, other, r):
        return at(y, other, z, r) if mode == 0 else at(other, x, z, r)

    def mine(mode):
        return x if mode == 0 else y

    def give(mode, d, n):
        dest = shift(mine(mode), d)
        send(
            send_bufs[mode].at[dest, n], recv_bufs[mode].at[mine(mode), n],
            ls_sem.at[mode, d, n], lrecv_sem.at[mode, mine(mode), n], place(mode, dest, g),
        )

    widen(1)
    pack(0, shift(x, 1))

    pl.semaphore_wait(barrier, len(peers))

    for m in (1, 0):
        for d in (1, 3, 2):
            begin(harmonics_copy(0, m, d, False))
    hg1[0][z] = harm[0][...]
    hg1[1][x] = harm[1][...]
    give(0, 1, 0)
    give(0, 1, 1)
    widen(3)
    pack(0, shift(x, 3))
    give(0, 3, 0)
    give(0, 3, 1)
    widen(2)
    widen(0)
    pack(1, shift(y, 1))
    give(1, 1, 0)
    pack(1, shift(y, 3))
    give(1, 3, 0)
    for m in (0, 1):
        for d in (1, 3, 2):
            harmonics_copy(0, m, d, True).wait_recv()
        for d in (1, 3, 2):
            begin(harmonics_copy(1, m, d, False))
    give(1, 1, 1)
    give(1, 3, 1)
    hg[0][y] = hg1[0][...]
    hg[1][:, z] = hg1[1][...]
    pack(0, shift(x, 2))
    give(0, 2, 0)
    give(0, 2, 1)
    pack(1, shift(y, 2))
    give(1, 2, 0)
    give(1, 2, 1)
    for mode in (1, 0):
        own = mine(mode)
        pack(mode, own)
        recv_bufs[mode][own] = send_bufs[mode][own]

    def digits(i, carry):
        col = pl.ds(pl.multiple_of((i // 4) * 256, 256), 256)
        who = i % 4
        used = (lax.broadcasted_iota(jnp.int32, (1, 256), 1) & 127) < 80
        hi = jnp.where(used, digs[who, :, col], -1.0).astype(jnp.int32)
        lo = digs[who + 8, :, col].astype(jnp.int32)
        pt[i] = jnp.where(
            lax.broadcasted_iota(jnp.int32, (40, 256), 0) == hi, 1.0, 0.0
        ).astype(F32)
        qt[i] = jnp.where(
            (lax.broadcasted_iota(jnp.int32, (128, 256), 0) & 63) == lo, 1.0, 0.0
        ).astype(BF16)
        return carry

    lax.fori_loop(0, 32, digits, 0)

    need("spread_t", "lane_sum")

    def parity(mode):
        line = row_of(rows16[...], 8 + mode * 4 + mine(mode)).astype(jnp.int32)
        return jnp.where((line & 1) == 1, -1.0, 1.0)

    full_acc[...] = jnp.zeros_like(full_acc)
    for m in range(2):
        for dd in (1, 3, 2):
            harmonics_copy(1, m, dd, True).wait_recv()
        width = PIECE[m] * 128
        for c in range(2):
            blocks = hg[m][:, :, c * 16 : c * 16 + 16, :].reshape(256, width)
            for c0 in range(0, width, 256):
                c1 = min(width, c0 + 256)
                hst[m, c * 240 : c * 240 + 240, c0:c1] = nn(spread_t[...], blocks[:, c0:c1])

    def synthesize(mode, src):
        tiles = (XT, YT)[mode]
        table = recv_bufs[mode]
        own = mine(mode)

        def group(i, carry):
            r0 = pl.multiple_of(i * 16, 16)
            rows = pl.ds(r0, 16)
            limit = thr[mode, own, rows, :]
            total = [[None, None], [None, None]]
            upper = [[None, None], [None, None]]
            for t in range(tiles):
                tile = t + (0 if mode == 0 else XT)
                is_a = limit <= 128 * tile
                for c in range(2):
                    row = pl.ds(pl.multiple_of((c * 3 + t // PIECE[mode]) * 80 + r0, 16), 16)
                    h = hst[mode, row, (t % PIECE[mode]) * 128 : (t % PIECE[mode]) * 128 + 128]
                    for n in range(2):
                        v = table[src, n, rows, t * 128 : t * 128 + 128].astype(F32) * h
                        w = jnp.where(is_a, v, 0.0)
                        total[n][c] = v if t == 0 else total[n][c] + v
                        upper[n][c] = w if t == 0 else upper[n][c] + w
            for n in range(2):
                for c in range(2):
                    accs[n, 2 * c, rows, :] = upper[n][c]
                    accs[n, 2 * c + 1, rows, :] = total[n][c] - upper[n][c]
            return carry

        lax.fori_loop(0, 5, group, 0)
        sign = parity(mode)
        signs = jnp.concatenate([sign] * 4, axis=1)
        for n in range(2):
            rows = accs[n].reshape(512, 128)
            hi = rows.astype(BF16)
            lo = (rows - hi.astype(F32)).astype(BF16)
            both = nt(lane_sum[...], jnp.concatenate([hi, lo], axis=1))
            fsend[mode, src, n] = both[0:1]
            fsend[mode, src, n + 2] = both[1:2] * signs

    def scatter(mode, d):
        own = mine(mode)
        p = shift(own, (4 - d) % 4)
        total = full_acc[...]
        for e in range(4):
            r = shift(g, e)
            if d or e:
                remote(
                    fsend.at[mode, p, r], frecv.at[mode, p, r],
                    fs_sem.at[mode, d, e], fr_sem.at[mode, p, r], at(y, x, z, g),
                ).wait_recv()
            i = mode * 16 + p * 4 + r
            row = frecv[mode, p, r]
            digit = pt[i]
            both = jnp.concatenate([digit * row[:, 0:256], digit * row[:, 256:512]], axis=0)
            hi = both.astype(BF16)
            lo = (both - hi.astype(F32)).astype(BF16)
            total = total + nt(jnp.concatenate([hi, lo], axis=0), qt[i])
        full_acc[...] = total

    behind = []
    for d in (0, 3, 1, 2):
        for mode in (1, 0):
            own = mine(mode)
            src = shift(own, d)
            if d:
                for n in range(2):
                    remote(
                        send_bufs[mode].at[src, n], recv_bufs[mode].at[src, n],
                        ls_sem.at[mode, d, n], lrecv_sem.at[mode, src, n], at(y, x, z, g),
                    ).wait_recv()
            synthesize(mode, src)
            for e in range(4):
                r = shift(g, e)
                if d or e:
                    send(
                        fsend.at[mode, src, r], frecv.at[mode, own, g],
                        fs_sem.at[mode, d, e], fr_sem.at[mode, own, g], place(mode, src, r),
                    )
                else:
                    frecv[mode, own, g] = fsend[mode, src, r]
            behind.append((mode, d))
            if len(behind) > 6:
                scatter(*behind.pop(0))
    for mode, d in behind:
        scatter(mode, d)

    need(*OPERANDS)
    h = g % 2

    def halves(v):
        hi = v.astype(BF16)
        return hi, (v - hi.astype(F32)).astype(BF16)

    def thrice(v, axis):
        hi, lo = halves(v)
        return jnp.concatenate([hi, hi, lo], axis=axis)

    full = full_acc[...]
    full = (full[0:80] + full[80:160]) * weight[...]
    section = nn(synth[h], thrice(full, 0))
    turned = section[0:128] * turn_a[h] + section[128:256] * turn_b[h]
    log_density = nt(fine_out[...], thrice(turned, 1))
    inside = msk[...].astype(F32)
    number = inside * cnt[...].astype(F32)
    dens = inside * jnp.exp(log_density)
    psend[0, 0] = jnp.concatenate(
        [jnp.sum(dens, axis=0, keepdims=True), jnp.sum(number, axis=0, keepdims=True)], axis=1
    )
    precv[0, x, g] = psend[0, 0]
    for d in range(4):
        for e in range(4):
            if d or e:
                send(
                    psend.at[0, 0], precv.at[0, x, g], ps_sem.at[0, d, e], pr_sem.at[0, x, g],
                    at(y, shift(x, d), z, shift(g, e)),
                )

    first = nn(fine_in[...], thrice(jnp.concatenate([number, dens], axis=1), 0))
    lines = []
    for f in range(2):
        re, im = first[0:64, f * 128 : f * 128 + 128], first[64:128, f * 128 : f * 128 + 128]
        tre = re * back_re[h] + im * back_im[h]
        tim = im * back_re[h] - re * back_im[h]
        line = thrice(jnp.concatenate([tre, tim], axis=1), 1)
        lines += [line, line]
    modes = nt(gather[h], jnp.concatenate(lines, axis=0))
    modes = jnp.concatenate([modes[:, 0:128] * weight[...], modes[:, 128:256] * weight[...]], axis=0)
    modes_hi = modes.astype(BF16).astype(F32)
    lane = lax.broadcasted_iota(jnp.int32, (160, 128), 1)
    modes = jnp.where(lane < 64, modes_hi, modes - modes_hi).astype(BF16)

    def second_sums():
        for d in range(4):
            for e in range(4):
                if d or e:
                    xx, gg = shift(x, d), shift(g, e)
                    remote(
                        psend.at[0, 0], precv.at[0, xx, gg], ps_sem.at[0, d, e], pr_sem.at[0, xx, gg],
                        at(y, x, z, g),
                    ).wait_recv()
        psend[1, 0] = jnp.sum(precv[0].reshape(16, 1, 256), axis=0)
        precv[1, y, z] = psend[1, 0]
        for d in range(4):
            for e in range(4):
                if d or e:
                    send(
                        psend.at[1, 0], precv.at[1, y, z], ps_sem.at[1, d, e], pr_sem.at[1, y, z],
                        at(shift(y, d), x, shift(z, e), g),
                    )

    for mode in (0, 1):
        own = mine(mode)
        if mode == 1:
            second_sums()
        for d in (2, 1, 3, 0):
            p = shift(own, d)
            for e in range(4):
                gg = shift(g, e)
                i = mode * 16 + p * 4 + gg
                rows = nn(modes, qt[i])
                digit = pt[i]
                for k in range(4):
                    line = jnp.sum(rows[k * 40 : k * 40 + 40] * digit, axis=0, keepdims=True)
                    for ab in range(2):
                        bsend[mode, p, gg, 2 * k + ab : 2 * k + ab + 1, :] = line[:, ab * 128 : ab * 128 + 128]
                if d or e:
                    send(
                        bsend.at[mode, p, gg], brecv.at[mode, own, g],
                        bs_sem.at[mode, d, e], br_sem.at[mode, own, g], place(mode, p, gg),
                    )
                else:
                    brecv[mode, own, g] = bsend[mode, p, gg]

    for d in range(4):
        for e in range(4):
            if d or e:
                yy, zz = shift(y, d), shift(z, e)
                remote(
                    psend.at[1, 0], precv.at[1, yy, zz], ps_sem.at[1, d, e], pr_sem.at[1, yy, zz],
                    at(y, x, z, g),
                ).wait_recv()
    sums = jnp.sum(precv[1].reshape(16, 1, 256), axis=0)
    ratio = jnp.sum(sums[:, 128:256], axis=1, keepdims=True) / jnp.sum(
        sums[:, 0:128], axis=1, keepdims=True
    )

    def coefficients(mode):
        own = mine(mode)
        for d in range(4):
            for e in range(4):
                if d or e:
                    p, r = shift(own, d), shift(g, e)
                    remote(
                        bsend.at[mode, p, r], brecv.at[mode, p, r],
                        bs_sem.at[mode, d, e], br_sem.at[mode, p, r], at(y, x, z, g),
                    ).wait_recv()
        sign = parity(mode)
        for p in range(4):
            lines = []
            for r in range(4):
                tile = brecv[mode, p, r]
                line = tile - ratio * pltpu.roll(tile, 4, 0)
                line = jnp.where(lax.broadcasted_iota(jnp.int32, (8, 128), 0) < 4, line, 0.0)
                lines.append(line if r < 2 else line * sign)
            across = nt(eye[...], jnp.concatenate(lines, axis=0).astype(BF16))
            coef[mode, p] = nn(across[0:80].astype(BF16), expand[...])

    def analyse(mode, c):
        tiles = (XT, YT)[mode]
        own = mine(mode)
        table = recv_bufs[mode]

        def group(i, carry):
            r0 = pl.multiple_of(i * 16, 16)
            rows = pl.ds(r0, 16)
            limit = thr[mode, own, rows, :]
            co = []
            for p in range(4):
                for n in range(2):
                    at_lane = ((n * 2 + c) * 2) * 128
                    co.append(
                        (
                            coef[mode, p, rows, at_lane : at_lane + 128],
                            coef[mode, p, rows, at_lane + 128 : at_lane + 256],
                        )
                    )
            for t in range(tiles):
                is_a = limit <= 128.0 * (t + (0 if mode == 0 else XT))
                total = None
                for p in range(4):
                    for n in range(2):
                        v = table[p, n, rows, t * 128 : t * 128 + 128].astype(F32) * jnp.where(
                            is_a, co[2 * p + n][0], co[2 * p + n][1]
                        )
                        total = v if total is None else total + v
                row = pl.ds(pl.multiple_of((c * 3 + t // PIECE[mode]) * 80 + r0, 16), 16)
                at_lane = (t % PIECE[mode]) * 128
                gst[mode][row, at_lane : at_lane + 128] = total.astype(BF16)
            return carry

        lax.fori_loop(0, 5, group, 0)
        across = y if mode == 0 else x
        for d in (1, 3, 2, 0):
            dest = shift(across, d)
            rows = pl.ds(pl.multiple_of(dest * 64, 64), 64)
            part = nn(spread[rows, :], gst[mode][c * 240 : c * 240 + 240, :]).astype(BF16)
            if d:
                gs1[mode][c, dest] = part
                begin(first_sum(mode, c, d, False))
            else:
                gr1[mode][c, across] = part

    def first_sum(mode, c, d, arriving):
        across = y if mode == 0 else x
        there = shift(across, d)
        slot = there if arriving else across
        who = at(there, x, z, g) if mode == 0 else at(y, there, z, g)
        return remote(
            gs1[mode].at[c, there], gr1[mode].at[c, slot], g1s.at[mode, c, d], g1r.at[mode, c, slot], who
        )

    def second_sum(mode, c, d, arriving):
        there = shift(z, d)
        slot = there if arriving else z
        return remote(
            gs2[mode].at[c, there], gr2[mode].at[c, slot], g2s.at[mode, c, d], g2r.at[mode, c, slot],
            at(y, x, there, g),
        )

    def sum4(ref, c):
        total = ref[c, 0].astype(F32)
        for k in range(1, 4):
            total = total + ref[c, k].astype(F32)
        return total

    for mode, c in ((0, 0), (1, 0), (0, 1), (1, 1)):
        if c == 0:
            coefficients(mode)
        analyse(mode, c)

    for mode, c in ((0, 0), (1, 0), (0, 1), (1, 1)):
        for d in (1, 3, 2):
            first_sum(mode, c, d, True).wait_recv()
        gs2[mode][c] = sum4(gr1[mode], c).astype(BF16).reshape(4, 16, PIECE[mode] * 128)
        for d in (2, 1, 3):
            begin(second_sum(mode, c, d, False))
        gr2[mode][c, z] = gs2[mode][c, z]
    tot[...] = jnp.zeros_like(tot)
    for mode, c in ((0, 0), (1, 0), (0, 1), (1, 1)):
        for d in (1, 3, 2):
            second_sum(mode, c, d, True).wait_recv()
        tot[mode, c * 16 : c * 16 + 16, 0 : PIECE[mode] * 128] = sum4(gr2[mode], c)

    own_order = own_limit - 128.0 + lax.broadcasted_iota(jnp.int32, (16, 128), 1).astype(F32)
    lane16 = lax.broadcasted_iota(jnp.int32, (16, 128), 1).astype(F32)
    for t in range(XT + YT):
        m, r0, c0 = where_packed(t)
        value = jnp.concatenate(
            [tot[m, c * 16 + r0 : c * 16 + r0 + 8, c0 : c0 + 128] for c in range(2)], axis=0
        )
        if t > 0:
            cols = slice((t - 1) * 128, t * 128)
            even = jnp.where(own_limit <= 128.0 * t, value, 0.0)
            for k in range(OWN):
                for c in range(2):
                    out[2 * k, c : c + 1, cols] = even[8 * c + k : 8 * c + k + 1]
        if t < XT + YT - 1:
            s = 19 - t
            cols = slice(s * 128, s * 128 + 128)
            hi = value.astype(BF16)
            lo = (value - hi.astype(F32)).astype(BF16)
            back = nn(hi, flip[128:256, 0:128]) + nn(lo, flip[128:256, 0:128])
            odd = jnp.where(own_order + lane16 >= 2559.0 - 128.0 * s, back, 0.0)
            for k in range(OWN):
                for c in range(2):
                    out[2 * k + 1, c : c + 1, cols] = odd[8 * c + k : 8 * c + k + 1]

    for c in pending:
        c.wait_send()


def per_device(white_noise, amplitude, legendre, order_of_slot, counts, survey_mask):
    tables = [jnp.asarray(t) for t in selection_tables()]
    operands = (
        [order_of_slot] + tables[:3] + [white_noise, amplitude] + tables[3:]
        + [jnp.asarray(t) for t in dft_tables()]
        + [counts.reshape(64, 128), survey_mask.reshape(64, 128)]
    )
    vmem = pl.BlockSpec(memory_space=pltpu.VMEM)
    dma = pltpu.SemaphoreType.DMA
    got = pl.pallas_call(
        kernel,
        out_shape=jax.ShapeDtypeStruct(white_noise.shape, F32),
        in_specs=[pl.BlockSpec(memory_space=pl.ANY)] * (1 + len(operands)),
        out_specs=vmem,
        scratch_shapes=[pltpu.VMEM(o.shape, o.dtype) for o in operands]
        + [
            dma((len(operands),)),
            pltpu.VMEM((2, 4, 4, 48, 2560), BF16),
            pltpu.VMEM((2, 20, 16, 56, 128), F32),
            pltpu.VMEM((4, 2, 80, LANES[0]), BF16),
            pltpu.VMEM((4, 2, 80, LANES[1]), BF16),
            pltpu.VMEM((4, 2, 80, LANES[0]), BF16),
            pltpu.VMEM((4, 2, 80, LANES[1]), BF16),
            pltpu.VMEM((4, 32, 512), BF16),
            pltpu.VMEM((4, 32, 384), BF16),
            pltpu.VMEM((4, 4, 32, 512), BF16),
            pltpu.VMEM((4, 4, 32, 384), BF16),
            pltpu.VMEM((2, 480, 512), F32),
            pltpu.VMEM((2, 4, 128, 128), F32),
            pltpu.VMEM((2, 4, 4, 1, 512), F32),
            pltpu.VMEM((2, 4, 4, 1, 512), F32),
            pltpu.VMEM((32, 40, 256), F32),
            pltpu.VMEM((32, 128, 256), BF16),
            pltpu.VMEM((2, 4, 4, 8, 128), F32),
            pltpu.VMEM((2, 4, 4, 8, 128), F32),
            pltpu.VMEM((2, 1, 1, 256), F32),
            pltpu.VMEM((2, 4, 4, 1, 256), F32),
            pltpu.VMEM((2, 4, 80, 1024), F32),
            pltpu.VMEM((480, 512), BF16),
            pltpu.VMEM((480, 384), BF16),
            pltpu.VMEM((2, 4, 64, 512), BF16),
            pltpu.VMEM((2, 4, 64, 384), BF16),
            pltpu.VMEM((2, 4, 64, 512), BF16),
            pltpu.VMEM((2, 4, 64, 384), BF16),
            pltpu.VMEM((2, 4, 16, 512), BF16),
            pltpu.VMEM((2, 4, 16, 384), BF16),
            pltpu.VMEM((2, 4, 16, 512), BF16),
            pltpu.VMEM((2, 4, 16, 384), BF16),
            pltpu.VMEM((16, 1, 2048), F32),
            pltpu.VMEM((16, 640), F32),
            pltpu.VMEM((2, 4, 80, 128), F32),
            pltpu.VMEM((16, 128), F32),
            pltpu.VMEM((16, 128), F32),
            pltpu.VMEM((16, 2560), F32),
            pltpu.VMEM((16, 2560), F32),
            pltpu.VMEM((2, 32, 512), F32),
            pltpu.VMEM((32, 512), BF16),
            pltpu.VMEM((32, 384), BF16),
            pltpu.VMEM((2, 40, 512), F32),
            pltpu.VMEM((160, 128), F32),
            dma((4, 2, 4)),
            dma((2, 4, 2)),
            dma((2, 4, 2)),
            dma((2, 4)),
            dma((2, 4)),
            dma((2, 4)),
            dma((2, 4)),
            dma((2, 4, 4)),
            dma((2, 4, 4)),
            dma((2, 4, 4)),
            dma((2, 4, 4)),
            dma((2, 4, 4)),
            dma((2, 4, 4)),
            dma((2, 2, 4)),
            dma((2, 2, 4)),
            dma((2, 2, 4)),
            dma((2, 2, 4)),
        ],
        compiler_params=pltpu.CompilerParams(
            collective_id=0, has_side_effects=True, vmem_limit_bytes=58 * 1024 * 1024
        ),
        name="survey",
    )(legendre, *operands)
    return got * amplitude


def solution(mesh):
    placed = (
        P(("ma", "blk"), None, None),
        P(),
        P("blk", "ma", None),
        P(),
        P(("blk", "ma"), None),
        P(("blk", "ma"), None),
    )
    return jax.shard_map(
        per_device,
        mesh=mesh,
        in_specs=placed,
        out_specs=P(("ma", "blk"), None, None),
        check_vma=False,
    )
```
